128 devices in a mesh: ctx: 32 (over y, x, core), fsdp: 4 (over z).
Axes of the slice: x: 4, y: 4, z: 4, core: 2. Of those that a mesh axis runs over, the one named last changes fastest.
Arguments:
- activations: bfloat16 [8, 4096, 960], P('fsdp', 'ctx'), may hold values from -6 to 6
- cotangent: bfloat16 [8, 4096, 960], P('fsdp', 'ctx'), may hold values from -6 to 6
- block_order: int32 [64], replicated, may hold values from 0 to 63, as said below
- attend_gain: bfloat16 [960], P('fsdp'), may hold values from 0.099609375 to 1.8984375
- query_weight: bfloat16 [960, 960], P('fsdp'), may hold values from -0.1875 to 0.1875
- key_weight: bfloat16 [960, 320], P('fsdp'), may hold values from -0.1875 to 0.1875
- value_weight: bfloat16 [960, 320], P('fsdp'), may hold values from -0.1875 to 0.1875
- output_weight: bfloat16 [960, 960], P('fsdp'), may hold values from -2 to 2
- dense_gain: bfloat16 [960], P('fsdp'), may hold values from 0.099609375 to 1.8984375
- gate_weight: bfloat16 [960, 2560], P('fsdp'), may hold values from -0.1875 to 0.1875
- up_weight: bfloat16 [960, 2560], P('fsdp'), may hold values from -0.1875 to 0.1875
- down_weight: bfloat16 [2560, 960], P('fsdp'), may hold values from -0.125 to 0.125
Outputs:
- layer_output: bfloat16 [8, 4096, 960], P('fsdp', 'ctx')
- input_grads: float32 [8, 4096, 960], P('fsdp', 'ctx')
- attend_gain_grads: float32 [960], P('fsdp')
- query_grads: float32 [960, 960], P('fsdp')
- key_grads: float32 [960, 320], P('fsdp')
- value_grads: float32 [960, 320], P('fsdp')
- output_grads: float32 [960, 960], P('fsdp')
- dense_gain_grads: float32 [960], P('fsdp')
- gate_grads: float32 [960, 2560], P('fsdp')
- up_grads: float32 [960, 2560], P('fsdp')
- down_grads: float32 [2560, 960], P('fsdp')
The draws below stay inside these ranges and needn't reach their ends.
Inputs may be any that keep to these rules, and one draw needn't show every extreme that they name: block_order is a permutation of 0 to 63 in which the entries 2 c and 2 c + 1 add up to 63 for every c.
All inputs are finite; a program needn't handle non-finite values.
Results may differ from the reference program's by a relative error of at most 0.03.
Values may be sent and summed in bfloat16 or wider, within the bound.
No kernel may reach another device: no remote copies, remote signals or barrier semaphores. Data moves between devices by JAX's collectives and lax.ppermute only.
A program may use at most 192 MiB of HBM per device.

```python
import jax
import jax.numpy as jnp
from jax import lax

D = 960
FF = 2560
HEADS = 15
KV_HEADS = 5
HEAD = 64
BLOCK = 512
GROUP = 3
HALF = 64
SEQ = 4096
SEQS = 8
BLOCKS = 64


def draw_block_order(key, part):
    key = jax.random.fold_in(key, 7)
    pick_key, turn_key = jax.random.split(key)
    lower = jax.random.permutation(pick_key, BLOCKS // 2).astype(jnp.int32)
    flipped = jax.random.randint(turn_key, (BLOCKS // 2,), 0, 2, dtype=jnp.int32)
    upper = BLOCKS - 1 - lower
    first = flipped * upper + (1 - flipped) * lower
    second = BLOCKS - 1 - first
    return jnp.stack([first, second], axis=1).reshape(BLOCKS).astype(jnp.int32)


def block_scale(own_key, dims, cuts, least, largest):
    gain, own = 1.0, jax.random.fold_in(own_key, 6)
    for position, blocks in cuts:
        draws = jnp.exp(jax.random.uniform(jax.random.fold_in(own, position), (blocks,), jnp.float32, least / len(cuts), largest / len(cuts)))
        gain = gain * jnp.repeat(draws, dims[position] // blocks).reshape([-1 if axis == position else 1 for axis in range(len(dims))])
    return gain


def gaussian(rng, shape, width, limit, shards=(), held_as=jnp.bfloat16):
    factor_of = block_scale(rng, shape, shards, -0.22, 0.18) if shards else 1.0
    values = jax.random.normal(rng, shape, jnp.float32) * width * factor_of
    return jnp.minimum(jnp.maximum(values, -limit), limit).astype(held_as)


def setup_inputs(seed: int = 0) -> dict:
    key_list = jax.random.split(jax.random.key(seed), 13)
    return {
        "activations": gaussian(key_list[0], (SEQS, SEQ, D), 1.0, 6.0, ((0, 4), (1, 32))),
        "cotangent": gaussian(key_list[1], (SEQS, SEQ, D), 1.0, 6.0, ((0, 4), (1, 32))),
        "block_order": draw_block_order(jax.random.fold_in(key_list[12], 71), 0),
        "attend_gain": jnp.clip(1.0 + 0.18 * jax.random.normal(key_list[3], (D,), jnp.float32), 0.099609375, 1.8984375).astype(jnp.bfloat16),
        "query_weight": gaussian(key_list[4], (D, D), D ** -0.5, 0.1875, ((0, 4),)),
        "key_weight": gaussian(key_list[5], (D, KV_HEADS * HEAD), D ** -0.5, 0.1875, ((0, 4),)),
        "value_weight": gaussian(key_list[6], (D, KV_HEADS * HEAD), D ** -0.5, 0.1875, ((0, 4),)),
        "output_weight": gaussian(key_list[7], (D, D), (max(D // 128, 1)) ** -0.5, 2.0, ((0, 4),)),
        "dense_gain": jnp.clip(1.0 + 0.18 * jax.random.normal(key_list[8], (D,), jnp.float32), 0.099609375, 1.8984375).astype(jnp.bfloat16),
        "gate_weight": gaussian(key_list[9], (D, FF), D ** -0.5, 0.1875, ((0, 4),)),
        "up_weight": gaussian(key_list[10], (D, FF), D ** -0.5, 0.1875, ((0, 4),)),
        "down_weight": gaussian(key_list[11], (FF, D), FF ** -0.5, 0.125, ((0, 4),)),
    }


@jax.custom_vjp
def low(v):
    return lax.optimization_barrier(v.astype(jnp.bfloat16)).astype(jnp.float32)

@jax.custom_vjp
def low_back(v):
    return v

def low_keep(v):
    return (low(v), None)

def low_pass(kept, grad):
    return (grad,)

def back_keep(v):
    return (v, None)

def back_low(kept, grad):
    return (low(grad),)
low.defvjp(low_keep, low_pass)
low_back.defvjp(back_keep, back_low)
EPSILON = 1e-05
THETA = 100000.0
SCALE = 0.125
MASKED = -1e+30

def rope_tables(places):
    pair_ids = jnp.arange(HEAD // 2, dtype=jnp.float32)
    frequency = THETA ** (-2.0 * pair_ids / HEAD)
    angles = places.astype(jnp.float32)[:, None] * frequency[None, :]
    angles = jnp.concatenate([angles, angles], axis=1)
    return (jnp.cos(angles), jnp.sin(angles))

def turn_half(heads):
    return jnp.concatenate([-heads[..., HEAD // 2:], heads[..., :HEAD // 2]], axis=-1)

def rotate(values, cosine, sine_table):
    row_count = values.shape[0]
    heads = values.reshape(row_count, -1, HEAD)
    turned = heads * cosine[:, None, :] + turn_half(heads) * sine_table[:, None, :]
    return turned.reshape(row_count, -1)

def matmul(left, right):
    return jnp.dot(left, right, precision=lax.Precision.HIGHEST)

def layer_forward(inputs, attend_gain, query_weight, key_weight, value_weight, output_weight, dense_gain, gate_weight, up_weight, down_weight, places, cosine, sine_table):
    scale_one = lax.rsqrt(lax.optimization_barrier(jnp.mean(inputs * inputs, axis=-1, keepdims=True)) + EPSILON)
    normed_one = low(inputs * scale_one * attend_gain)
    queries = low(rotate(low_back(matmul(normed_one, query_weight)), cosine, sine_table))
    key_rows = low(rotate(low_back(matmul(normed_one, key_weight)), cosine, sine_table))
    values = low(low_back(matmul(normed_one, value_weight)))
    query_heads = queries.reshape(SEQ, KV_HEADS, GROUP, HEAD)
    key_heads = key_rows.reshape(SEQ, KV_HEADS, HEAD)
    value_heads = values.reshape(SEQ, KV_HEADS, HEAD)

    def score_block(block_index):
        first_row = block_index * BLOCK
        query_block = lax.dynamic_slice_in_dim(query_heads, first_row, BLOCK, 0)
        query_places = lax.dynamic_slice_in_dim(places, first_row, BLOCK, 0)
        raw_scores = jnp.einsum('qkgd,skd->kgqs', query_block, key_heads, precision=lax.Precision.HIGHEST) * SCALE
        allowed = places[None, :] <= query_places[:, None]
        scores = jnp.where(allowed[None, None], low_back(raw_scores), MASKED)
        highest = lax.optimization_barrier(jnp.max(scores, axis=-1, keepdims=True))
        log_total = highest + jnp.log(lax.optimization_barrier(jnp.sum(jnp.exp(scores - highest), axis=-1, keepdims=True)))
        weights_soft = low(jnp.exp(scores - log_total))
        block_output = jnp.einsum('kgqs,skd->qkgd', weights_soft, value_heads, precision=lax.Precision.HIGHEST)
        return block_output.reshape(BLOCK, HEADS * HEAD)
    attended = lax.map(jax.checkpoint(score_block), jnp.arange(SEQ // BLOCK, dtype=jnp.int32))
    attended = low(low_back(attended.reshape(SEQ, HEADS * HEAD)))
    middle = inputs + low_back(matmul(attended, output_weight))
    scale_two = lax.rsqrt(lax.optimization_barrier(jnp.mean(middle * middle, axis=-1, keepdims=True)) + EPSILON)
    normed_two = low(middle * scale_two * dense_gain)
    gate_rows = low_back(matmul(normed_two, gate_weight))
    upper = low_back(matmul(normed_two, up_weight))
    hidden = low(jax.nn.silu(gate_rows) * upper)
    return middle + low_back(matmul(hidden, down_weight))

def reference(activations, cotangent, block_order, attend_gain, query_weight, key_weight, value_weight, output_weight, dense_gain, gate_weight, up_weight, down_weight):
    row_ids = jnp.arange(SEQ, dtype=jnp.int32)
    places = block_order[row_ids // HALF].astype(jnp.int32) * HALF + row_ids % HALF
    cosine, sine_table = rope_tables(places)
    weights = tuple((matrix.astype(jnp.float32) for matrix in (attend_gain, query_weight, key_weight, value_weight, output_weight, dense_gain, gate_weight, up_weight, down_weight)))

    def sequence_step(running, sequence_pair):
        inputs, grad_rows = sequence_pair

        def forward(inputs_float, *params):
            return layer_forward(inputs_float, *params, places, cosine, sine_table)
        output, pullback = jax.vjp(forward, inputs.astype(jnp.float32), *weights)
        gradients = pullback(grad_rows.astype(jnp.float32))
        running = tuple((total_sum + addend for total_sum, addend in zip(running, gradients[1:])))
        return (running, (output.astype(jnp.bfloat16), gradients[0]))
    starting = tuple((jnp.zeros(matrix.shape, jnp.float32) for matrix in weights))
    totals, (outputs, input_grads) = lax.scan(sequence_step, starting, (activations, cotangent))
    return (outputs, input_grads, totals[0], totals[1], totals[2], totals[3], totals[4], totals[5], totals[6], totals[7], totals[8])
```

```python
import functools

import jax
import jax.numpy as jnp
import numpy as np
from jax import lax
from jax.experimental import pallas as pl
from jax.experimental.pallas import tpu as pltpu
from jax.sharding import PartitionSpec as P

D = 960
FF = 2560
HEADS = 15
KV_HEADS = 5
GROUP = 3
HEAD = 64
HALF = 64
CHUNK = 256
SIDE = 4
KV = KV_HEADS * 128
PROJ = KV + D
PART = 832
PART_AT = PROJ - PART
SHARD = D // SIDE
PADDED = 256
SLICE = FF // SIDE
EPSILON = 1e-05
THETA = 100000.0
SCALE = 0.125
MASKED = -1e30
F32 = jnp.float32
BF16 = jnp.bfloat16
NN = (((1,), (0,)), ((), ()))
NT = (((1,), (1,)), ((), ()))
TN = (((0,), (0,)), ((), ()))
LIMIT = 52 * 2**20
SMEM = pl.BlockSpec(memory_space=pltpu.SMEM)
VMEM = pl.BlockSpec(memory_space=pltpu.VMEM)


def dot(left, right, dims=NN):
    return lax.dot_general(left, right, dims, preferred_element_type=F32)


def call(kernel, name, out_shape, inputs, in_specs, scratch=()):
    return pl.pallas_call(
        kernel,
        out_shape=out_shape,
        in_specs=in_specs,
        out_specs=jax.tree.map(lambda _: VMEM, out_shape),
        scratch_shapes=list(scratch),
        compiler_params=pltpu.CompilerParams(vmem_limit_bytes=LIMIT),
        name=name,
    )(*inputs)


def ctx_index(y, x, core):
    return (y * SIDE + x) * 2 + core


def plane_pairs(step, first_turn):
    pairs = []
    for y in range(SIDE):
        for x in range(SIDE):
            for core in range(2):
                along_x = (core == 0) == first_turn
                target = (y, (x + step) % SIDE) if along_x else ((y + step) % SIDE, x)
                pairs.append((ctx_index(y, x, core), ctx_index(*target, core)))
    return pairs


def z_move(step):
    pairs = [(z, (z + step) % SIDE) for z in range(SIDE)]
    return lambda rows: lax.ppermute(rows, "fsdp", pairs)


def plane_move(step, first_turn):
    pairs = plane_pairs(step, first_turn)
    return lambda rows: lax.ppermute(rows, "ctx", pairs)


def core_swap(rows):
    pairs = [(index, index ^ 1) for index in range(2 * SIDE * SIDE)]
    return lax.ppermute(rows, "ctx", pairs)


Z_RING = (z_move(1), z_move(-1), z_move(2))
FIRST_RING = (plane_move(1, True), plane_move(-1, True), plane_move(2, True))
SECOND_RING = (plane_move(1, False), plane_move(-1, False), plane_move(2, False))


def ring_gather(rows, ring):
    plus, minus, _ = ring
    half = rows.shape[0] // 2
    before, after = plus(rows), minus(rows)
    return rows, before, after, plus(before[:half]), minus(after[half:])


def add_low(left, right):
    return (left.astype(F32) + right.astype(F32)).astype(BF16)


def ring_scatter(own, before, after, opposite_top, opposite_low, ring):
    plus, minus, _ = ring
    half = own.shape[0] // 2
    to_before, to_after = minus(opposite_top), plus(opposite_low)
    before = jnp.concatenate([add_low(before[:half], to_before), before[half:]], axis=0)
    after = jnp.concatenate([after[:half], add_low(after[half:], to_after)], axis=0)
    return own.astype(F32) + minus(before).astype(F32) + plus(after).astype(F32)


def slot_table():
    devices = 2 * SIDE * SIDE
    held = {i: [2 * i, 2 * i + 1, 2 * (i ^ 1), 2 * (i ^ 1) + 1] for i in range(devices)}
    own = {i: list(held[i]) for i in held}
    for turn in (True, False):
        source = {step: {t: s for s, t in plane_pairs(step, turn)} for step in (1, -1, 2)}
        grown = {}
        for i in held:
            half = len(held[i]) // 2
            opposite = held[source[2][i]]
            grown[i] = (
                held[i] + held[source[1][i]] + held[source[-1][i]] + opposite[:half] + opposite[half:]
            )
        held = grown
    table = np.array([held[i] for i in range(devices)], np.int32)
    assert all((table[i, :4] == own[i]).all() for i in range(devices))
    return table


def pack_kernel(core_ref, q_ref, k_ref, v_ref, gains_ref, mine_ref, other_ref):
    columns = []
    for head in range(KV_HEADS):
        at = slice(head * HEAD, (head + 1) * HEAD)
        columns += [k_ref[:, at], v_ref[:, at]]
    columns.append(q_ref[...])
    packed = jnp.concatenate(columns, axis=1)
    low, high = packed[:, :PART], packed[:, PART_AT:]
    is_low = core_ref[0] == 0
    mine_ref[:SHARD, :] = jnp.where(is_low, low, high)
    other_ref[:SHARD, :] = jnp.where(is_low, high, low)
    mine_ref[SHARD:, :] = gains_ref[...]
    other_ref[SHARD:, :] = gains_ref[...]


def rope(values, cosine, sine, back):
    lane = lax.broadcasted_iota(jnp.int32, values.shape, 1)
    first = (lane & (HEAD - 1)) < HEAD // 2
    turned = values * sine if back else values
    ahead, behind = pltpu.roll(turned, 128 - HEAD // 2, 1), pltpu.roll(turned, HEAD // 2, 1)
    if back:
        return values * cosine + jnp.where(first, ahead, -behind)
    return values * cosine + jnp.where(first, -ahead, behind) * sine


def half_tables(cosine, sine):
    lane = lax.broadcasted_iota(jnp.int32, cosine.shape, 1)
    return jnp.where(lane < HEAD, cosine, 1.0), jnp.where(lane < HEAD, sine, 0.0)


def project_kernel(
    where_ref, x_mine, x_got, cosine_ref, sine_ref, *refs
):
    pieces, (q_ref, kv_ref, normed_ref, weight_ref, gains_ref, result) = refs[:10], refs[10:]
    z, core = where_ref[0], where_ref[1]
    mine_at = pl.multiple_of(core * PART_AT, 128)
    other_at = pl.multiple_of((1 - core) * PART_AT, 128)
    gains = jnp.zeros((16, 512), F32)
    for turn, place in enumerate((z, (z + 3) & 3, (z + 1) & 3)):
        at = pl.multiple_of(place * SHARD, 16)
        for piece, column in ((pieces[2 * turn], mine_at), (pieces[2 * turn + 1], other_at)):
            weight_ref[pl.ds(at, SHARD), pl.ds(column, PART)] = piece[:SHARD, :]
        gains += pieces[2 * turn][SHARD:, :512].astype(F32)
    at = pl.multiple_of(((z + 2) & 3) * SHARD, 16)
    for top, low, column in ((pieces[6], pieces[8], mine_at), (pieces[7], pieces[9], other_at)):
        weight_ref[pl.ds(at, 128), pl.ds(column, PART)] = top[...]
        weight_ref[pl.ds(at + 128, SHARD - 128), pl.ds(column, PART)] = low[: SHARD - 128, :]
    gains += pieces[8][SHARD - 128 :, :512].astype(F32)
    wide = jnp.concatenate(
        [
            jnp.concatenate([gains[0:1], gains[1:2]], axis=1),
            jnp.concatenate([gains[2:3], gains[3:4]], axis=1),
        ],
        axis=0,
    )[:, :D]
    gains_ref[...] = wide
    rows = x_mine.shape[0]
    for half, x_ref in enumerate((x_mine, x_got)):
        x = x_ref[...].astype(F32)
        scale = lax.rsqrt(jnp.mean(x * x, axis=-1, keepdims=True) + EPSILON)
        normed_ref[half * rows : (half + 1) * rows, :] = (x * scale * wide[0:1]).astype(BF16)
    result[...] = dot(normed_ref[...], weight_ref[...])
    cosine, sine = cosine_ref[...], sine_ref[...]
    kv_tables = half_tables(cosine, sine)
    for head in range(KV_HEADS):
        at = slice(head * 128, (head + 1) * 128)
        kv_ref[:, at] = rope(result[:, at], *kv_tables, False).astype(BF16)
    for tile in range(D // 128):
        at = slice(tile * 128, (tile + 1) * 128)
        turned = rope(result[:, KV + tile * 128 : KV + (tile + 1) * 128], cosine, sine, False)
        q_ref[:, at] = (turned.astype(BF16) * SCALE).astype(BF16)
    tail = jnp.concatenate([result[:, PROJ - HEAD :]] * 2, axis=1)
    q_ref[:, D - HEAD :] = (rope(tail, cosine, sine, False)[:, :HEAD].astype(BF16) * SCALE).astype(
        BF16
    )


def sort_rows(order_ref, sources, sorted_ref):
    first = 0
    for source in sources:

        def step(slot, carry, source=source, first=first):
            place = order_ref[first + slot]
            sorted_ref[pl.ds(pl.multiple_of(place * HALF, HALF), HALF), :] = source[
                pl.ds(pl.multiple_of(slot * HALF, HALF), HALF), :
            ]
            return carry

        count = source.shape[0] // HALF
        lax.fori_loop(0, count, step, 0)
        first += count


def allowed_mask(chunk, place, rows):
    key_at = lax.broadcasted_iota(jnp.int32, (rows, CHUNK), 1) + chunk * CHUNK
    query_at = (lax.broadcasted_iota(jnp.int32, (rows, CHUNK), 0) & (HALF - 1)) + place * HALF
    return key_at <= query_at


def packed_queries(rows_ref, block, kv_head, upper):
    parts = []
    for member in range(GROUP):
        head = kv_head * GROUP + member
        part = rows_ref[block * HALF : (block + 1) * HALF, head * HEAD : (head + 1) * HEAD]
        zero = jnp.zeros_like(part)
        parts.append(jnp.concatenate([zero, part] if upper else [part, zero], axis=1))
    return jnp.concatenate(parts, axis=0)


def attend_kernel(blocks, parts, order_ref, q_ref, *refs):
    sources, (o_ref, ox_ref, lse_ref, kvs, qx, scores, tops) = refs[:parts], refs[parts:]
    rows = GROUP * HALF
    sort_rows(order_ref, sources, kvs)
    for block in range(blocks):
        for k in range(KV_HEADS):
            qx[block, k] = packed_queries(q_ref, block, k, False)

    def one_block(block, carry):
        place = order_ref[block]
        last = place >> 2
        tops[...] = jnp.full(tops.shape, MASKED, F32)

        def score_chunk(chunk, masked):
            at = pl.ds(pl.multiple_of(chunk * CHUNK, CHUNK), CHUNK)
            if masked:
                mask = allowed_mask(chunk, place, rows)
            for k in range(KV_HEADS):
                s = dot(qx[block, k], kvs[at, k * 128 : (k + 1) * 128], NT)
                if masked:
                    s = jnp.where(mask, s, MASKED)
                scores[k, chunk] = s
                tops[k] = jnp.maximum(tops[k], jnp.maximum(s[:, :128], s[:, 128:]))

        def score_step(chunk, c):
            score_chunk(chunk, False)
            return c

        lax.fori_loop(0, last, score_step, 0)
        score_chunk(last, True)
        for k in range(KV_HEADS):
            top = jnp.max(tops[k], axis=1, keepdims=True)
            tops[k] = jnp.broadcast_to(top, (rows, 128))
            lse_ref[block, k] = jnp.zeros((rows, 128), F32)
            ox_ref[block, k] = jnp.zeros((rows, 128), F32)

        def out_step(chunk, c):
            at = pl.ds(pl.multiple_of(chunk * CHUNK, CHUNK), CHUNK)
            for k in range(KV_HEADS):
                top = tops[k]
                s = scores[k, chunk]
                p0 = jnp.exp(s[:, :128] - top)
                p1 = jnp.exp(s[:, 128:] - top)
                lse_ref[block, k] += p0 + p1
                p = jnp.concatenate([p0, p1], axis=1).astype(BF16)
                ox_ref[block, k] += dot(p, kvs[at, k * 128 : (k + 1) * 128])
            return c

        lax.fori_loop(0, last + 1, out_step, 0)
        for k in range(KV_HEADS):
            total = jnp.sum(lse_ref[block, k], axis=1, keepdims=True)
            ox_ref[block, k] = ox_ref[block, k] / total
            lse_ref[block, k] = tops[k] + jnp.log(total)
        return carry

    lax.fori_loop(0, blocks, one_block, 0)
    for block in range(blocks):
        pieces = [
            ox_ref[block, k, g * HALF : (g + 1) * HALF, HEAD:].astype(BF16)
            for k in range(KV_HEADS)
            for g in range(GROUP)
        ]
        o_ref[block * HALF : (block + 1) * HALF, :] = jnp.concatenate(pieces, axis=1)


def attend(order, q, sources):
    length = sum(source.shape[0] for source in sources)
    blocks = q.shape[0] // HALF
    rows = GROUP * HALF
    packed = jax.ShapeDtypeStruct((blocks, KV_HEADS, rows, 128), F32)
    return call(
        functools.partial(attend_kernel, blocks, len(sources)),
        "attend",
        (jax.ShapeDtypeStruct(q.shape, BF16), packed, packed),
        (order, q, *sources),
        [SMEM] + [VMEM] * (1 + len(sources)),
        [
            pltpu.VMEM((length, KV), BF16),
            pltpu.VMEM((blocks, KV_HEADS, rows, 128), BF16),
            pltpu.VMEM((KV_HEADS, length // CHUNK, rows, CHUNK), F32),
            pltpu.VMEM((KV_HEADS, rows, 128), F32),
        ],
    )


def attend_back_kernel(blocks, parts, order_ref, q_ref, g_ref, ox_ref, lse_ref, *refs):
    sources, refs = refs[:parts], refs[parts:]
    dq_ref, refs = refs[0], refs[1:]
    results, (kvs, qg, qgt, dots, dqx, dkvt) = refs[:parts], refs[parts:]
    rows = GROUP * HALF
    sort_rows(order_ref, sources, kvs)
    for block in range(blocks):
        for k in range(KV_HEADS):
            q = packed_queries(q_ref, block, k, False)
            g = packed_queries(g_ref, block, k, True)
            qg[block, k, :rows, :] = q
            qg[block, k, rows:, :] = g
            both = jnp.concatenate([q, g], axis=0).astype(F32)
            qgt[block, k] = both.T.astype(BF16)
            summed = jnp.sum(g.astype(F32) * ox_ref[block, k], axis=1, keepdims=True)
            dots[block, k] = jnp.broadcast_to(summed, (rows, 128))
    dqx[...] = jnp.zeros(dqx.shape, F32)

    def clear(chunk, c):
        dkvt[chunk] = jnp.zeros(dkvt.shape[1:], F32)
        return c

    lax.fori_loop(0, dkvt.shape[0], clear, 0)

    def one_block(block, carry):
        place = order_ref[block]
        last = place >> 2

        def chunk_work(chunk, masked):
            at = pl.ds(pl.multiple_of(chunk * CHUNK, CHUNK), CHUNK)
            if masked:
                mask = allowed_mask(chunk, place, rows)
            for k in range(KV_HEADS):
                keys = kvs[at, k * 128 : (k + 1) * 128]
                both = dot(qg[block, k], keys, NT)
                lse = lse_ref[block, k]
                dots_here = dots[block, k]
                ps, ds = [], []
                for half in range(2):
                    lanes = slice(half * 128, (half + 1) * 128)
                    p = jnp.exp(both[:rows, lanes] - lse)
                    if masked:
                        p = jnp.where(mask[:, lanes], p, 0.0)
                    ps.append(p.astype(BF16))
                    ds.append((p * (both[rows:, lanes] - dots_here)).astype(BF16))
                p = jnp.concatenate(ps, axis=1)
                d = jnp.concatenate(ds, axis=1)
                dqx[block, k] += dot(d, keys)
                dkvt[chunk, k] += dot(qgt[block, k], jnp.concatenate([d, p], axis=0))

        def step(chunk, c):
            chunk_work(chunk, False)
            return c

        lax.fori_loop(0, last, step, 0)
        chunk_work(last, True)
        return carry

    lax.fori_loop(0, blocks, one_block, 0)
    for block in range(blocks):
        pieces = [
            dqx[block, k, g * HALF : (g + 1) * HALF, :HEAD] * SCALE
            for k in range(KV_HEADS)
            for g in range(GROUP)
        ]
        dq_ref[block * HALF : (block + 1) * HALF, :] = jnp.concatenate(pieces, axis=1)

    def turn(chunk, c):
        at = pl.ds(pl.multiple_of(chunk * CHUNK, CHUNK), CHUNK)
        for k in range(KV_HEADS):
            kvs[at, k * 128 : (k + 1) * 128] = dkvt[chunk, k].T.astype(BF16)
        return c

    lax.fori_loop(0, dkvt.shape[0], turn, 0)
    first = 0
    for result in results:

        def unsort(slot, c, result=result, first=first):
            place = order_ref[first + slot]
            result[pl.ds(pl.multiple_of(slot * HALF, HALF), HALF), :] = kvs[
                pl.ds(pl.multiple_of(place * HALF, HALF), HALF), :
            ]
            return c

        count = result.shape[0] // HALF
        lax.fori_loop(0, count, unsort, 0)
        first += count


def attend_back(order, q, g, ox, lse, sources):
    length = sum(source.shape[0] for source in sources)
    blocks = q.shape[0] // HALF
    rows = GROUP * HALF
    return call(
        functools.partial(attend_back_kernel, blocks, len(sources)),
        "attend_back",
        (jax.ShapeDtypeStruct(q.shape, F32),)
        + tuple(jax.ShapeDtypeStruct(source.shape, BF16) for source in sources),
        (order, q, g, ox, lse, *sources),
        [SMEM] + [VMEM] * (4 + len(sources)),
        [
            pltpu.VMEM((length, KV), BF16),
            pltpu.VMEM((blocks, KV_HEADS, 2 * rows, 128), BF16),
            pltpu.VMEM((blocks, KV_HEADS, 128, 2 * rows), BF16),
            pltpu.VMEM((blocks, KV_HEADS, rows, 128), F32),
            pltpu.VMEM((blocks, KV_HEADS, rows, 128), F32),
            pltpu.VMEM((length // CHUNK, KV_HEADS, 128, CHUNK), F32),
        ],
    )


def query_back_kernel(dq_ref, cosine_ref, sine_ref, low_ref):
    cosine, sine = cosine_ref[...], sine_ref[...]
    for tile in range(D // 128):
        at = slice(tile * 128, (tile + 1) * 128)
        low_ref[:, at] = rope(dq_ref[:, at], cosine, sine, True).astype(BF16)
    tail = jnp.concatenate([dq_ref[:, D - HEAD :]] * 2, axis=1)
    low_ref[:, D - HEAD :] = rope(tail, cosine, sine, True)[:, :HEAD].astype(BF16)


def input_back_kernel(
    x_mine, x_got, dkv_ref, q_low_ref, cosine_ref, sine_ref, weight_ref, gains_ref, middle_ref,
    low_ref, grads_ref, gain_ref,
):
    kv_tables = half_tables(cosine_ref[...], sine_ref[...])
    for head in range(KV_HEADS):
        at = slice(head * 128, (head + 1) * 128)
        low_ref[:, at] = rope(dkv_ref[:, at], *kv_tables, True).astype(BF16)
    low_ref[:, KV:] = q_low_ref[...]
    back = dot(low_ref[...], weight_ref[...], NT)
    rows = x_mine.shape[0]
    gain = gains_ref[0:1, :]
    total = jnp.zeros((1, D), F32)
    for half, x_ref in enumerate((x_mine, x_got)):
        at = slice(half * rows, (half + 1) * rows)
        x = x_ref[...].astype(F32)
        scale = lax.rsqrt(jnp.mean(x * x, axis=-1, keepdims=True) + EPSILON)
        unit = x * scale
        total += jnp.sum(back[at] * unit, axis=0, keepdims=True)
        weighted = back[at] * gain
        inner = jnp.mean(weighted * unit, axis=-1, keepdims=True)
        grads_ref[at, :] = middle_ref[at, :] + scale * (weighted - unit * inner)
    gain_ref[...] = total


def rope_tables(places):
    pair_ids = jnp.arange(HEAD // 2, dtype=F32)
    frequency = THETA ** (-2.0 * pair_ids / HEAD)
    angles = places.astype(F32)[:, None] * frequency[None, :]
    return jnp.tile(jnp.cos(angles), (1, 4)), jnp.tile(jnp.sin(angles), (1, 4))


def norm_back(grad_normed, values, scale, gain):
    unit_rows = values * scale
    gain_grad = jnp.sum(grad_normed * unit_rows, axis=0)
    weighted = grad_normed * gain
    inner = jnp.mean(weighted * unit_rows, axis=-1, keepdims=True)
    return gain_grad, scale * (weighted - unit_rows * inner)


def after(value, *others):
    return lax.optimization_barrier((value, *others))[0]


def rows_at(array, block, size):
    return lax.dynamic_slice_in_dim(array, block * size, size, 0)


def assemble(pieces, places, axis):
    size = pieces[0].shape[axis]
    shape = list(pieces[0].shape)
    shape[axis] = size * len(pieces)
    whole = jnp.zeros(shape, pieces[0].dtype)
    for piece, place in zip(pieces, places):
        whole = lax.dynamic_update_slice_in_dim(whole, piece, place * size, axis)
    return whole


def local(
    activations, cotangent, block_order, attend_gain, query_weight, key_weight, value_weight,
    output_weight, dense_gain, gate_weight, up_weight, down_weight,
):
    index = lax.axis_index("ctx")
    z = lax.axis_index("fsdp")
    core = index & 1
    tokens = activations.shape[1]
    rows = 2 * tokens
    ring_places = (z, (z + 3) & 3, (z + 1) & 3, (z + 2) & 3)

    x_mine = lax.dynamic_index_in_dim(activations, core, 0, False)
    x_got = core_swap(lax.dynamic_index_in_dim(activations, 1 - core, 0, False))

    gains = jnp.stack(
        [
            lax.dynamic_update_slice_in_dim(jnp.zeros((1024,), BF16), gain, z * SHARD, 0)
            for gain in (attend_gain, dense_gain)
        ]
    ).reshape(4, 512)
    gains = jnp.pad(gains, ((0, 12), (0, PART - 512)))
    shape = jax.ShapeDtypeStruct((PADDED, PART), BF16)
    mine, other = call(
        pack_kernel, "pack", (shape, shape),
        (core.reshape(1).astype(jnp.int32), query_weight, key_weight, value_weight, gains),
        [SMEM] + [VMEM] * 4,
    )
    ringed = ring_gather(mine, Z_RING)
    pieces = [mine, other]
    for piece in ringed[1:]:
        pieces += [piece, core_swap(piece)]

    slots = jnp.asarray(slot_table())[index]
    order = jnp.sum(
        jnp.where(slots[:, None] == jnp.arange(64, dtype=jnp.int32)[None, :], block_order[None, :], 0),
        axis=1,
    )
    places = (order[: rows // HALF, None] * HALF + jnp.arange(HALF, dtype=jnp.int32)).reshape(rows)
    cosine, sine = rope_tables(places)
    queries, kv, normed_one, weight, gain_rows = call(
        project_kernel,
        "project",
        (
            jax.ShapeDtypeStruct((rows, D), BF16),
            jax.ShapeDtypeStruct((rows, KV), BF16),
            jax.ShapeDtypeStruct((rows, D), BF16),
            jax.ShapeDtypeStruct((D, PROJ), BF16),
            jax.ShapeDtypeStruct((2, D), F32),
        ),
        (jnp.stack([z, core]).astype(jnp.int32), x_mine, x_got, cosine, sine, *pieces),
        [SMEM] + [VMEM] * 14,
        [pltpu.VMEM((rows, PROJ), F32)],
    )

    line = jnp.concatenate(ring_gather(kv, FIRST_RING), axis=0)
    sources = ring_gather(line, SECOND_RING)

    cotangent, output_weight, gate_weight, up_weight = lax.optimization_barrier(
        (cotangent, output_weight, gate_weight, up_weight, kv)
    )[:4]
    wo = lax.all_gather(output_weight, "fsdp", axis=0, tiled=True)
    g_mine = lax.dynamic_index_in_dim(cotangent, core, 0, False)
    g_got = core_swap(lax.dynamic_index_in_dim(cotangent, 1 - core, 0, False))
    g_own = jnp.concatenate([g_mine, g_got], axis=0)
    g_rows = jnp.concatenate(ring_gather(g_own, Z_RING), axis=0)

    def columns_for(place):
        return jnp.concatenate(
            [
                lax.dynamic_slice_in_dim(w, place * SLICE, SLICE, 1)
                for w in (gate_weight, up_weight)
            ],
            axis=1,
        )

    came = (
        columns_for(z),
        Z_RING[0](columns_for((z + 1) & 3)),
        Z_RING[1](columns_for((z + 3) & 3)),
        Z_RING[2](columns_for((z + 2) & 3)),
    )
    gate_up = assemble(came, ring_places, 0)
    normed_swapped = core_swap(normed_one)

    attended, ox, lse = attend(order, queries, sources)

    x = jnp.concatenate([x_mine, x_got], axis=0).astype(F32)
    middle = x + dot(attended, wo)
    gain_two = gain_rows[1]
    scale_two = lax.rsqrt(jnp.mean(middle * middle, axis=-1, keepdims=True) + EPSILON)
    normed_two = (middle * scale_two * gain_two).astype(BF16)

    n_rows = jnp.concatenate(ring_gather(normed_two, Z_RING), axis=0)
    gate_rows = dot(n_rows, gate_up[:, :SLICE])
    upper = dot(n_rows, gate_up[:, SLICE:])
    sigmoid_gate = jax.nn.sigmoid(gate_rows)
    hidden = (gate_rows * sigmoid_gate * upper).astype(BF16)
    grad_hidden = dot(g_rows, down_weight, NT)
    grad_gate = (
        grad_hidden * upper * sigmoid_gate * (1.0 + gate_rows * (1.0 - sigmoid_gate))
    ).astype(BF16)
    grad_upper = (grad_hidden * gate_rows * sigmoid_gate).astype(BF16)
    grad_both = jnp.concatenate([grad_gate, grad_upper], axis=1)
    grad_normed = dot(grad_both, gate_up, NT).astype(BF16)

    def split(array):
        half = rows // 2
        cuts = [0, rows, 2 * rows, 3 * rows, 3 * rows + half, 4 * rows]
        return [array[a:b] for a, b in zip(cuts[:-1], cuts[1:])]

    grad_normed_two = ring_scatter(*split(grad_normed), Z_RING)
    dense_gain_grad, norm_two_back = norm_back(grad_normed_two, middle, scale_two, gain_two)
    grad_middle = g_own.astype(F32) + norm_two_back
    grad_branch = grad_middle.astype(BF16)
    grad_attended = dot(grad_branch, wo, NT).astype(BF16)

    dq, *dkv = attend_back(order, queries, grad_attended, ox, lse, sources)

    low_grad_attended = grad_attended
    hidden, n_rows, grad_both = after((hidden, n_rows, grad_both), low_grad_attended)
    down_rows = dot(hidden, down_weight).astype(BF16)
    down_grad = dot(hidden, g_rows, TN).astype(BF16)
    both_grad = dot(n_rows, grad_both, TN).astype(BF16)
    output_grad = dot(attended, grad_branch, TN).astype(BF16)
    came = (
        rows_at(both_grad, z, SHARD),
        Z_RING[0](rows_at(both_grad, (z + 1) & 3, SHARD)),
        Z_RING[1](rows_at(both_grad, (z + 3) & 3, SHARD)),
        Z_RING[2](rows_at(both_grad, (z + 2) & 3, SHARD)),
    )
    gate_grad = assemble([piece[:, :SLICE] for piece in came], ring_places, 1)
    up_grad = assemble([piece[:, SLICE:] for piece in came], ring_places, 1)
    blocks = [rows_at(output_grad, place, SHARD) for place in ring_places]
    output_grad = ring_scatter(
        *blocks[:3], blocks[3][: SHARD // 2], blocks[3][SHARD // 2 :], Z_RING
    ).astype(BF16)
    dense_grads = lax.psum((output_grad, gate_grad, up_grad, down_grad), "ctx")
    layer_rows = (middle + ring_scatter(*split(down_rows), Z_RING)).astype(BF16)

    line = ring_scatter(*dkv, SECOND_RING).astype(BF16)
    dkv_own = ring_scatter(*split(line), FIRST_RING)
    q_low = call(
        query_back_kernel, "query_back", jax.ShapeDtypeStruct((rows, D), BF16),
        (dq, cosine, sine), [VMEM] * 3,
    )
    low, input_rows, attend_gain_grad = call(
        input_back_kernel,
        "input_back",
        (
            jax.ShapeDtypeStruct((rows, PROJ), BF16),
            jax.ShapeDtypeStruct((rows, D), F32),
            jax.ShapeDtypeStruct((1, D), F32),
        ),
        (x_mine, x_got, dkv_own, q_low, cosine, sine, weight, gain_rows, grad_middle),
        [VMEM] * 9,
    )

    mine_at, other_at = core * PART_AT, (1 - core) * PART_AT
    low_mine = lax.dynamic_slice_in_dim(low, mine_at, PART, 1)
    low_got = core_swap(lax.dynamic_slice_in_dim(low, other_at, PART, 1))
    part_grad = dot(normed_one, low_mine, TN) + dot(normed_swapped, low_got, TN)
    gain_grads = jnp.concatenate([attend_gain_grad, dense_gain_grad[None, :]], axis=0)

    def part_for(place):
        row = lax.dynamic_slice_in_dim(gain_grads, place * SHARD, SHARD, 1)
        row = jnp.pad(row, ((0, PADDED - SHARD - 2), (0, PART - SHARD)))
        return jnp.concatenate([rows_at(part_grad, place, SHARD), row], axis=0).astype(BF16)

    blocks = [part_for(place) for place in ring_places]
    part = ring_scatter(*blocks[:3], blocks[3][:128], blocks[3][128:], Z_RING).astype(BF16)
    y, x_at = index >> 3, (index >> 1) & 3
    first_place = jnp.where(core == 0, x_at, y)
    quarters = [rows_at(part, (first_place + step) & 3, PADDED // 4) for step in (0, 3, 1, 2)]
    quarter = ring_scatter(*quarters[:3], quarters[3][:32], quarters[3][32:], FIRST_RING).astype(BF16)
    quarter_sum = quarter.astype(F32)
    for move in SECOND_RING:
        quarter_sum += move(quarter).astype(F32)
    quarter = quarter_sum.astype(BF16)
    part = assemble(
        [quarter] + [move(quarter) for move in FIRST_RING],
        [(first_place + step) & 3 for step in (0, 3, 1, 2)],
        0,
    )
    part_got = core_swap(part)
    is_low = core == 0
    low_part = jnp.where(is_low, part, part_got)
    high_part = jnp.where(is_low, part_got, part)
    gain_total = part[SHARD : SHARD + 2, :SHARD].astype(F32) + part_got[SHARD : SHARD + 2, :SHARD].astype(F32)
    kv_grad = low_part[:SHARD, :KV].astype(F32).reshape(SHARD, KV_HEADS, 2, HEAD)
    query_grad = jnp.concatenate(
        [low_part[:SHARD, KV:PART], high_part[:SHARD, PART - PART_AT :]], axis=1
    ).astype(F32)

    def back_to_cores(array):
        keep, give = array[:tokens], array[tokens:]
        got = core_swap(give)
        return jnp.where(is_low, jnp.stack([keep, got]), jnp.stack([got, keep]))

    output_grad, gate_grad, up_grad, down_grad = dense_grads
    return (
        back_to_cores(layer_rows),
        back_to_cores(input_rows.astype(BF16)).astype(F32),
        gain_total[0],
        query_grad,
        kv_grad[:, :, 0].reshape(SHARD, KV_HEADS * HEAD),
        kv_grad[:, :, 1].reshape(SHARD, KV_HEADS * HEAD),
        output_grad.astype(F32),
        gain_total[1],
        gate_grad.astype(F32),
        up_grad.astype(F32),
        down_grad.astype(F32),
    )


def solution(mesh):
    tokens = P("fsdp", "ctx", None)
    gain, weight = P("fsdp"), P("fsdp", None)
    weights = (gain, weight, weight, weight, weight, gain, weight, weight, weight)
    return jax.shard_map(
        local,
        mesh=mesh,
        in_specs=(tokens, tokens, P()) + weights,
        out_specs=(tokens, tokens) + weights,
        check_vma=False,
    )
```

```python
import functools

import jax
import jax.numpy as jnp
import numpy as np
from jax import lax
from jax.experimental import pallas as pl
from jax.experimental.pallas import tpu as pltpu
from jax.sharding import PartitionSpec as P

D = 960
FF = 2560
HEADS = 15
KV_HEADS = 5
GROUP = 3
HEAD = 64
HALF = 64
CHUNK = 256
SIDE = 4
KV = KV_HEADS * 128
PROJ = KV + D
PART = 832
PART_AT = PROJ - PART
SHARD = D // SIDE
PADDED = 256
SLICE = FF // SIDE
SIDE_COLUMNS = 384
SIDE_AT = KV - SIDE_COLUMNS
EPSILON = 1e-05
THETA = 100000.0
SCALE = 0.125
MASKED = -1e30
F32 = jnp.float32
BF16 = jnp.bfloat16
NN = (((1,), (0,)), ((), ()))
NT = (((1,), (1,)), ((), ()))
TN = (((0,), (0,)), ((), ()))
LIMIT = 52 * 2**20
SMEM = pl.BlockSpec(memory_space=pltpu.SMEM)
VMEM = pl.BlockSpec(memory_space=pltpu.VMEM)


def dot(left, right, dims=NN):
    return lax.dot_general(left, right, dims, preferred_element_type=F32)


def call(kernel, name, out_shape, inputs, in_specs, scratch=(), flops=10**9):
    return pl.pallas_call(
        kernel,
        out_shape=out_shape,
        in_specs=in_specs,
        out_specs=jax.tree.map(lambda _: VMEM, out_shape),
        scratch_shapes=list(scratch),
        compiler_params=pltpu.CompilerParams(vmem_limit_bytes=LIMIT),
        cost_estimate=pl.CostEstimate(flops=flops, bytes_accessed=0 if flops == 0 else 2**20, transcendentals=0),
        name=name,
    )(*inputs)


def join_kernel(*refs):
    first = 0
    for ref in refs[:-1]:
        refs[-1][first : first + ref.shape[0], :] = ref[...]
        first += ref.shape[0]


def join(pieces):
    rows = sum(piece.shape[0] for piece in pieces)
    shape = jax.ShapeDtypeStruct((rows, pieces[0].shape[1]), pieces[0].dtype)
    return call(join_kernel, "join", shape, tuple(pieces), [VMEM] * len(pieces))


def ctx_index(y, x, core):
    return (y * SIDE + x) * 2 + core


def plane_pairs(step, first_turn):
    pairs = []
    for y in range(SIDE):
        for x in range(SIDE):
            for core in range(2):
                along_x = (core == 0) == first_turn
                target = (y, (x + step) % SIDE) if along_x else ((y + step) % SIDE, x)
                pairs.append((ctx_index(y, x, core), ctx_index(*target, core)))
    return pairs


def z_move(step):
    pairs = [(z, (z + step) % SIDE) for z in range(SIDE)]
    return lambda rows: lax.ppermute(rows, "fsdp", pairs)


def plane_move(step, first_turn):
    pairs = plane_pairs(step, first_turn)
    return lambda rows: lax.ppermute(rows, "ctx", pairs)


def core_swap(rows):
    pairs = [(index, index ^ 1) for index in range(2 * SIDE * SIDE)]
    return lax.ppermute(rows, "ctx", pairs)


Z_RING = (z_move(1), z_move(-1), z_move(2))
FIRST_RING = (plane_move(1, True), plane_move(-1, True), plane_move(2, True))
SECOND_RING = (plane_move(1, False), plane_move(-1, False), plane_move(2, False))


def ring_gather(rows, ring):
    plus, minus, _ = ring
    half = rows.shape[0] // 2
    before, after = plus(rows), minus(rows)
    return rows, before, after, plus(before[:half]), minus(after[half:])


def direct_gather(rows, ring):
    return (rows, *(move(rows) for move in ring))


def add_low(left, right):
    return (left.astype(F32) + right.astype(F32)).astype(BF16)


def scatter_sends(opposite_top, opposite_low, ring):
    return ring[1](opposite_top), ring[0](opposite_low)


def scatter_adds(own, before, after_it, to_before, to_after):
    half = own.shape[0] // 2
    before = jnp.concatenate([add_low(before[:half], to_before), before[half:]], axis=0)
    after_it = jnp.concatenate([after_it[:half], add_low(after_it[half:], to_after)], axis=0)
    return own, before, after_it


def scatter_start(own, before, after_it, opposite_top, opposite_low, ring):
    return scatter_adds(own, before, after_it, *scatter_sends(opposite_top, opposite_low, ring))


def scatter_end(terms, ring):
    own, before, after_it = terms
    return own.astype(F32) + ring[1](before).astype(F32) + ring[0](after_it).astype(F32)


def ring_scatter(own, before, after_it, opposite_top, opposite_low, ring):
    return scatter_end(scatter_start(own, before, after_it, opposite_top, opposite_low, ring), ring)


def slot_table():
    devices = 2 * SIDE * SIDE
    held = {i: [2 * i, 2 * i + 1, 2 * (i ^ 1), 2 * (i ^ 1) + 1] for i in range(devices)}
    own = {i: list(held[i]) for i in held}
    for turn in (True, False):
        source = {step: {t: s for s, t in plane_pairs(step, turn)} for step in (1, -1, 2)}
        grown = {}
        for i in held:
            half = len(held[i]) // 2
            opposite = held[source[2][i]]
            grown[i] = (
                held[i] + held[source[1][i]] + held[source[-1][i]] + opposite[:half] + opposite[half:]
            )
        held = grown
    table = np.array([held[i] for i in range(devices)], np.int32)
    assert all((table[i, :4] == own[i]).all() for i in range(devices))
    return table


def pack_kernel(core_ref, q_ref, k_ref, v_ref, gain_one_ref, gain_two_ref, mine_ref, other_ref):
    columns = []
    for head in range(KV_HEADS):
        at = slice(head * HEAD, (head + 1) * HEAD)
        columns += [k_ref[:, at], v_ref[:, at]]
    columns.append(q_ref[...])
    packed = jnp.concatenate(columns, axis=1)
    low, high = packed[:, :PART], packed[:, PART_AT:]
    is_low = core_ref[0] == 0
    mine_ref[:SHARD, :] = jnp.where(is_low, low, high)
    other_ref[:SHARD, :] = jnp.where(is_low, high, low)
    rows = [gain_one_ref[...], gain_two_ref[...], jnp.zeros((PADDED - SHARD - 2, SHARD), BF16)]
    gains = jnp.concatenate([row.astype(F32) for row in rows], axis=0).astype(BF16)
    gains = jnp.concatenate([gains, jnp.zeros((PADDED - SHARD, PART - SHARD), BF16)], axis=1)
    mine_ref[SHARD:, :] = gains
    other_ref[SHARD:, :] = gains


def rope(values, cosine, sine, back):
    lane = lax.broadcasted_iota(jnp.int32, values.shape, 1)
    first = (lane & (HEAD - 1)) < HEAD // 2
    turned = values * sine if back else values
    ahead, behind = pltpu.roll(turned, 128 - HEAD // 2, 1), pltpu.roll(turned, HEAD // 2, 1)
    if back:
        return values * cosine + jnp.where(first, ahead, -behind)
    return values * cosine + jnp.where(first, -ahead, behind) * sine


def half_tables(cosine, sine):
    lane = lax.broadcasted_iota(jnp.int32, cosine.shape, 1)
    return jnp.where(lane < HEAD, cosine, 1.0), jnp.where(lane < HEAD, sine, 0.0)


def project_kernel(
    where_ref, x_mine, x_got, cosine_ref, sine_ref, *refs
):
    pieces, (q_ref, kv_ref, normed_ref, weight_ref, gains_ref, result) = refs[:10], refs[10:]
    z, core = where_ref[0], where_ref[1]
    mine_at = pl.multiple_of(core * PART_AT, 128)
    other_at = pl.multiple_of((1 - core) * PART_AT, 128)
    came = []
    for turn, place in enumerate((z, (z + 3) & 3, (z + 1) & 3)):
        at = pl.multiple_of(place * SHARD, 16)
        for piece, column in ((pieces[2 * turn], mine_at), (pieces[2 * turn + 1], other_at)):
            weight_ref[pl.ds(at, SHARD), pl.ds(column, PART)] = piece[:SHARD, :]
        came.append((place, pieces[2 * turn][SHARD:, :SHARD].astype(F32)))
    at = pl.multiple_of(((z + 2) & 3) * SHARD, 16)
    for top, low, column in ((pieces[6], pieces[8], mine_at), (pieces[7], pieces[9], other_at)):
        weight_ref[pl.ds(at, 128), pl.ds(column, PART)] = top[...]
        weight_ref[pl.ds(at + 128, SHARD - 128), pl.ds(column, PART)] = low[: SHARD - 128, :]
    came.append(((z + 2) & 3, pieces[8][SHARD - 128 :, :SHARD].astype(F32)))
    wide = jnp.concatenate(
        [sum(jnp.where(at == place, gain, 0.0) for at, gain in came) for place in range(SIDE)], axis=1
    )[:2]
    gains_ref[...] = wide
    rows = x_mine.shape[0]
    for half, x_ref in enumerate((x_mine, x_got)):
        x = x_ref[...].astype(F32)
        scale = lax.rsqrt(jnp.mean(x * x, axis=-1, keepdims=True) + EPSILON)
        normed_ref[half * rows : (half + 1) * rows, :] = (x * scale * wide[0:1]).astype(BF16)
    result[...] = dot(normed_ref[...], weight_ref[...])
    cosine, sine = cosine_ref[...], sine_ref[...]
    kv_tables = half_tables(cosine, sine)
    for head in range(KV_HEADS):
        at = slice(head * 128, (head + 1) * 128)
        kv_ref[:, at] = rope(result[:, at], *kv_tables, False).astype(BF16)
    for tile in range(D // 128):
        at = slice(tile * 128, (tile + 1) * 128)
        turned = rope(result[:, KV + tile * 128 : KV + (tile + 1) * 128], cosine, sine, False)
        q_ref[:, at] = (turned.astype(BF16) * SCALE).astype(BF16)
    tail = jnp.concatenate([result[:, PROJ - HEAD :]] * 2, axis=1)
    q_ref[:, D - HEAD :] = (rope(tail, cosine, sine, False)[:, :HEAD].astype(BF16) * SCALE).astype(
        BF16
    )


def sort_rows(order_ref, sources, sorted_ref):
    first = 0
    for source in sources:

        def step(slot, carry, source=source, first=first):
            place = order_ref[first + slot]
            sorted_ref[pl.ds(pl.multiple_of(place * HALF, HALF), HALF), :] = source[
                pl.ds(pl.multiple_of(slot * HALF, HALF), HALF), :
            ]
            return carry

        count = source.shape[0] // HALF
        lax.fori_loop(0, count, step, 0)
        first += count


def allowed_mask(chunk, place, rows):
    key_at = lax.broadcasted_iota(jnp.int32, (rows, CHUNK), 1) + chunk * CHUNK
    query_at = (lax.broadcasted_iota(jnp.int32, (rows, CHUNK), 0) & (HALF - 1)) + place * HALF
    return key_at <= query_at


def packed_queries(rows_ref, block, kv_head, upper):
    parts = []
    for member in range(GROUP):
        head = kv_head * GROUP + member
        part = rows_ref[block * HALF : (block + 1) * HALF, head * HEAD : (head + 1) * HEAD]
        zero = jnp.zeros_like(part)
        parts.append(jnp.concatenate([zero, part] if upper else [part, zero], axis=1))
    return jnp.concatenate(parts, axis=0)


def attend_kernel(blocks, parts, order_ref, q_ref, *refs):
    sources, (o_ref, ox_ref, lse_ref, kvs, qx, scores, tops) = refs[:parts], refs[parts:]
    rows = GROUP * HALF
    sort_rows(order_ref, sources, kvs)
    for block in range(blocks):
        for k in range(KV_HEADS):
            qx[block, k] = packed_queries(q_ref, block, k, False)

    def one_block(block, carry):
        place = order_ref[block]
        last = place >> 2
        tops[...] = jnp.full(tops.shape, MASKED, F32)

        def score_chunk(chunk, masked):
            at = pl.ds(pl.multiple_of(chunk * CHUNK, CHUNK), CHUNK)
            if masked:
                mask = allowed_mask(chunk, place, rows)
            for k in range(KV_HEADS):
                s = dot(qx[block, k], kvs[at, k * 128 : (k + 1) * 128], NT)
                if masked:
                    s = jnp.where(mask, s, MASKED)
                scores[k, chunk] = s
                tops[k] = jnp.maximum(tops[k], jnp.maximum(s[:, :128], s[:, 128:]))

        def score_step(chunk, c):
            score_chunk(chunk, False)
            return c

        lax.fori_loop(0, last, score_step, 0)
        score_chunk(last, True)
        for k in range(KV_HEADS):
            top = jnp.max(tops[k], axis=1, keepdims=True)
            tops[k] = jnp.broadcast_to(top, (rows, 128))
            lse_ref[block, k] = jnp.zeros((rows, 128), F32)
            ox_ref[block, k] = jnp.zeros((rows, 128), F32)

        def out_step(chunk, c):
            at = pl.ds(pl.multiple_of(chunk * CHUNK, CHUNK), CHUNK)
            for k in range(KV_HEADS):
                top = tops[k]
                s = scores[k, chunk]
                p0 = jnp.exp(s[:, :128] - top)
                p1 = jnp.exp(s[:, 128:] - top)
                lse_ref[block, k] += p0 + p1
                p = jnp.concatenate([p0, p1], axis=1).astype(BF16)
                ox_ref[block, k] += dot(p, kvs[at, k * 128 : (k + 1) * 128])
            return c

        lax.fori_loop(0, last + 1, out_step, 0)
        for k in range(KV_HEADS):
            total = jnp.sum(lse_ref[block, k], axis=1, keepdims=True)
            ox_ref[block, k] = ox_ref[block, k] / total
            lse_ref[block, k] = tops[k] + jnp.log(total)
        return carry

    lax.fori_loop(0, blocks, one_block, 0)
    for block in range(blocks):
        pieces = [
            ox_ref[block, k, g * HALF : (g + 1) * HALF, HEAD:].astype(BF16)
            for k in range(KV_HEADS)
            for g in range(GROUP)
        ]
        o_ref[block * HALF : (block + 1) * HALF, :] = jnp.concatenate(pieces, axis=1)


def attend(order, q, sources):
    length = sum(source.shape[0] for source in sources)
    blocks = q.shape[0] // HALF
    rows = GROUP * HALF
    packed = jax.ShapeDtypeStruct((blocks, KV_HEADS, rows, 128), F32)
    return call(
        functools.partial(attend_kernel, blocks, len(sources)),
        "attend",
        (jax.ShapeDtypeStruct(q.shape, BF16), packed, packed),
        (order, q, *sources),
        [SMEM] + [VMEM] * (1 + len(sources)),
        [
            pltpu.VMEM((length, KV), BF16),
            pltpu.VMEM((blocks, KV_HEADS, rows, 128), BF16),
            pltpu.VMEM((KV_HEADS, length // CHUNK, rows, CHUNK), F32),
            pltpu.VMEM((KV_HEADS, rows, 128), F32),
        ],
        3 * 10**10,
    )


def attend_back_kernel(
    blocks, parts, order_ref, q_ref, g_ref, ox_ref, lse_ref, *refs
):
    sources, refs = refs[:parts], refs[parts:]
    dq_ref, refs = refs[0], refs[1:]
    results, (kvs, qg, qgt, dots, dqx, dkvt) = refs[:parts], refs[parts:]
    rows = GROUP * HALF
    sort_rows(order_ref, sources, kvs)
    for block in range(blocks):
        for k in range(KV_HEADS):
            q = packed_queries(q_ref, block, k, False)
            g = packed_queries(g_ref, block, k, True)
            qg[block, k, :rows, :] = q
            qg[block, k, rows:, :] = g
            both = jnp.concatenate([q, g], axis=0).astype(F32)
            qgt[block, k] = both.T.astype(BF16)
            summed = jnp.sum(g.astype(F32) * ox_ref[block, k], axis=1, keepdims=True)
            dots[block, k] = jnp.broadcast_to(summed, (rows, 128))
    dqx[...] = jnp.zeros(dqx.shape, F32)

    def clear(chunk, c):
        dkvt[chunk] = jnp.zeros(dkvt.shape[1:], F32)
        return c

    lax.fori_loop(0, dkvt.shape[0], clear, 0)

    def one_block(block, carry):
        place = order_ref[block]
        last = place >> 2

        def chunk_work(chunk, masked):
            at = pl.ds(pl.multiple_of(chunk * CHUNK, CHUNK), CHUNK)
            if masked:
                mask = allowed_mask(chunk, place, rows)
            for k in range(KV_HEADS):
                keys = kvs[at, k * 128 : (k + 1) * 128]
                both = dot(qg[block, k], keys, NT)
                lse = lse_ref[block, k]
                dots_here = dots[block, k]
                ps, ds = [], []
                for half in range(2):
                    lanes = slice(half * 128, (half + 1) * 128)
                    p = jnp.exp(both[:rows, lanes] - lse)
                    if masked:
                        p = jnp.where(mask[:, lanes], p, 0.0)
                    ps.append(p.astype(BF16))
                    ds.append((p * (both[rows:, lanes] - dots_here)).astype(BF16))
                p = jnp.concatenate(ps, axis=1)
                d = jnp.concatenate(ds, axis=1)
                dqx[block, k] += dot(d, keys)
                dkvt[chunk, k] += dot(qgt[block, k], jnp.concatenate([d, p], axis=0))

        def step(chunk, c):
            chunk_work(chunk, False)
            return c

        lax.fori_loop(0, last, step, 0)
        chunk_work(last, True)
        return carry

    lax.fori_loop(0, blocks, one_block, 0)
    for block in range(blocks):
        pieces = [
            dqx[block, k, g * HALF : (g + 1) * HALF, :HEAD] * SCALE
            for k in range(KV_HEADS)
            for g in range(GROUP)
        ]
        dq_ref[block * HALF : (block + 1) * HALF, :] = jnp.concatenate(pieces, axis=1)

    def turn(chunk, c):
        at = pl.ds(pl.multiple_of(chunk * CHUNK, CHUNK), CHUNK)
        for k in range(KV_HEADS):
            kvs[at, k * 128 : (k + 1) * 128] = dkvt[chunk, k].T.astype(BF16)
        return c

    lax.fori_loop(0, dkvt.shape[0], turn, 0)
    first = 0
    for result in results:

        def unsort(slot, c, result=result, first=first):
            place = order_ref[first + slot]
            result[pl.ds(pl.multiple_of(slot * HALF, HALF), HALF), :] = kvs[
                pl.ds(pl.multiple_of(place * HALF, HALF), HALF), :
            ]
            return c

        count = result.shape[0] // HALF
        lax.fori_loop(0, count, unsort, 0)
        first += count


def attend_back(order, q, g, ox, lse, sources):
    length = sum(source.shape[0] for source in sources)
    blocks = q.shape[0] // HALF
    rows = GROUP * HALF
    return call(
        functools.partial(attend_back_kernel, blocks, len(sources)),
        "attend_back",
        (jax.ShapeDtypeStruct(q.shape, F32),)
        + tuple(jax.ShapeDtypeStruct(source.shape, BF16) for source in sources),
        (order, q, g, ox, lse, *sources),
        [SMEM] + [VMEM] * (4 + len(sources)),
        [
            pltpu.VMEM((length, KV), BF16),
            pltpu.VMEM((blocks, KV_HEADS, 2 * rows, 128), BF16),
            pltpu.VMEM((blocks, KV_HEADS, 128, 2 * rows), BF16),
            pltpu.VMEM((blocks, KV_HEADS, rows, 128), F32),
            pltpu.VMEM((blocks, KV_HEADS, rows, 128), F32),
            pltpu.VMEM((length // CHUNK, KV_HEADS, 128, CHUNK), F32),
        ],
        0,
    )


def query_back_kernel(dq_ref, cosine_ref, sine_ref, low_ref):
    cosine, sine = cosine_ref[...], sine_ref[...]
    for tile in range(D // 128):
        at = slice(tile * 128, (tile + 1) * 128)
        low_ref[:, at] = rope(dq_ref[:, at], cosine, sine, True).astype(BF16)
    tail = jnp.concatenate([dq_ref[:, D - HEAD :]] * 2, axis=1)
    low_ref[:, D - HEAD :] = rope(tail, cosine, sine, True)[:, :HEAD].astype(BF16)


def kv_back_kernel(dkv_ref, cosine_ref, sine_ref, low_ref):
    kv_tables = half_tables(cosine_ref[...], sine_ref[...])
    for head in range(KV_HEADS):
        at = slice(head * 128, (head + 1) * 128)
        low_ref[:, at] = rope(dkv_ref[:, at], *kv_tables, True).astype(BF16)


def input_back_kernel(
    x_mine, x_got, kv_low_ref, q_low_ref, weight_ref, gains_ref, middle_ref, grads_ref
):
    back = dot(kv_low_ref[...], weight_ref[:, :KV], NT) + dot(q_low_ref[...], weight_ref[:, KV:], NT)
    rows = x_mine.shape[0]
    gain = gains_ref[0:1, :]
    for half, x_ref in enumerate((x_mine, x_got)):
        at = slice(half * rows, (half + 1) * rows)
        x = x_ref[...].astype(F32)
        scale = lax.rsqrt(jnp.mean(x * x, axis=-1, keepdims=True) + EPSILON)
        unit = x * scale
        weighted = back[at] * gain
        inner = jnp.mean(weighted * unit, axis=-1, keepdims=True)
        grads_ref[at, :] = middle_ref[at, :] + scale * (weighted - unit * inner)


def place_kernel(own_ref, *refs):
    for piece, step in zip(refs[:-1], (0, 3, 1, 2)):
        rows = piece.shape[0]
        at = pl.multiple_of(((own_ref[0] + step) & 3) * rows, 16)
        refs[-1][pl.ds(at, rows), :] = piece[...]


def place_rows(pieces, own):
    rows, columns = pieces[0].shape
    shape = jax.ShapeDtypeStruct((SIDE * rows, columns), pieces[0].dtype)
    return call(
        place_kernel, "place", shape, (own.reshape(1).astype(jnp.int32), *pieces), [SMEM] + [VMEM] * 4
    )


def finish_kernel(
    core_ref, square_ref, square_got_ref, side_ref, side_got_ref, query_weight_ref, key_weight_ref,
    value_weight_ref, gain_ref, query_ref, key_ref, value_ref, output_ref, total_ref,
):
    is_low = core_ref[0] == 0
    mine, got = square_ref[:SHARD, :].astype(F32), square_got_ref[:SHARD, :].astype(F32)
    query = jnp.where(is_low, mine, got)
    query_ref[...] = query
    output_ref[...] = jnp.where(is_low, got, mine)
    mine, got = side_ref[...].astype(F32), side_got_ref[...].astype(F32)
    low, high = jnp.where(is_low, mine, got), jnp.where(is_low, got, mine)
    pairs = [low[:, at : at + 128] for at in range(0, SIDE_COLUMNS, 128)]
    pairs += [high[:, at : at + 128] for at in range(2 * SIDE_COLUMNS - KV, SIDE_COLUMNS, 128)]
    key = jnp.concatenate([pair[:, :HEAD] for pair in pairs], axis=1)
    value = jnp.concatenate([pair[:, HEAD:] for pair in pairs], axis=1)
    key_ref[...] = key
    value_ref[...] = value
    total = jnp.zeros((SHARD, 1), F32)
    for weight, grad in ((query_weight_ref, query), (key_weight_ref, key), (value_weight_ref, value)):
        total += jnp.sum(weight[...].astype(F32) * grad, axis=1, keepdims=True)
    total_ref[...] = jnp.broadcast_to(total, (SHARD, 128)) / gain_ref[...]


def unpack_kernel(
    z_ref, sums_ref, gate_weight_ref, up_weight_ref, gain_ref, gate_ref, up_ref, down_ref, dense_ref
):
    z = z_ref[0]
    for turn, step in enumerate((0, 3, 1, 2)):
        at = pl.ds(pl.multiple_of(((z + step) & 3) * SLICE, 128), SLICE)
        first = turn * 2 * SLICE
        gate_ref[:, at] = sums_ref[:SHARD, first : first + SLICE].astype(F32)
        up_ref[:, at] = sums_ref[:SHARD, first + SLICE : first + 2 * SLICE].astype(F32)
        columns = slice(2 * FF + turn * SLICE, 2 * FF + (turn + 1) * SLICE)
        down_ref[turn * SHARD : (turn + 1) * SHARD, :] = sums_ref[:SHARD, columns].astype(F32)
    terms = gate_weight_ref[...].astype(F32) * gate_ref[...] + up_weight_ref[...].astype(F32) * up_ref[...]
    total = jnp.sum(terms, axis=1, keepdims=True)
    dense_ref[...] = jnp.broadcast_to(total, (SHARD, 128)) / gain_ref[...]


def rope_angles(places):
    pair_ids = jnp.arange(HEAD // 2, dtype=F32)
    frequency = THETA ** (-2.0 * pair_ids / HEAD)
    return places.astype(F32)[:, None] * frequency[None, :]


def rope_tables(places):
    angles = rope_angles(places)
    return jnp.tile(jnp.cos(angles), (1, 4)), jnp.tile(jnp.sin(angles), (1, 4))


def norm_back(grad_normed, values, scale, gain):
    unit_rows = values * scale
    weighted = grad_normed * gain
    inner = jnp.mean(weighted * unit_rows, axis=-1, keepdims=True)
    return scale * (weighted - unit_rows * inner)


def together(*groups):
    return lax.optimization_barrier(groups)


def after(values, *others):
    return lax.optimization_barrier((tuple(values), others))[0]


def rows_at(array, block, size):
    return lax.dynamic_slice_in_dim(array, block * size, size, 0)


def local(
    activations, cotangent, block_order, attend_gain, query_weight, key_weight, value_weight,
    output_weight, dense_gain, gate_weight, up_weight, down_weight,
):
    index = lax.axis_index("ctx")
    z = lax.axis_index("fsdp")
    core = index & 1
    tokens = activations.shape[1]
    rows = 2 * tokens
    ring_places = (z, (z + 3) & 3, (z + 1) & 3, (z + 2) & 3)

    x_mine = lax.dynamic_index_in_dim(activations, core, 0, False)
    x_got = core_swap(lax.dynamic_index_in_dim(activations, 1 - core, 0, False))

    shape = jax.ShapeDtypeStruct((PADDED, PART), BF16)
    mine, other = call(
        pack_kernel, "pack", (shape, shape),
        (
            core.reshape(1).astype(jnp.int32), query_weight, key_weight, value_weight,
            attend_gain.reshape(1, SHARD), dense_gain.reshape(1, SHARD),
        ),
        [SMEM] + [VMEM] * 5,
    )
    ringed = ring_gather(mine, Z_RING)
    pieces = [mine, other]
    for piece in ringed[1:]:
        pieces += [piece, core_swap(piece)]

    slots = jnp.asarray(slot_table())[index]
    order = jnp.sum(
        jnp.where(slots[:, None] == jnp.arange(64, dtype=jnp.int32)[None, :], block_order[None, :], 0),
        axis=1,
    )
    places = (order[: rows // HALF, None] * HALF + jnp.arange(HALF, dtype=jnp.int32)).reshape(rows)
    cosine, sine = rope_tables(places)
    queries, kv, normed_one, weight, gain_rows = call(
        project_kernel,
        "project",
        (
            jax.ShapeDtypeStruct((rows, D), BF16),
            jax.ShapeDtypeStruct((rows, KV), BF16),
            jax.ShapeDtypeStruct((rows, D), BF16),
            jax.ShapeDtypeStruct((D, PROJ), BF16),
            jax.ShapeDtypeStruct((2, D), F32),
        ),
        (jnp.stack([z, core]).astype(jnp.int32), x_mine, x_got, cosine, sine, *pieces),
        [SMEM] + [VMEM] * 14,
        [pltpu.VMEM((rows, PROJ), F32)],
        5 * 10**9,
    )

    is_low = core == 0
    y, x_at = index >> 3, (index >> 1) & 3
    first_place = jnp.where(is_low, x_at, y)
    line_places = [(first_place + step) & 3 for step in (0, 3, 1, 2)]

    cotangent, output_weight, gate_weight, up_weight = after(
        (cotangent, output_weight, gate_weight, up_weight), kv
    )
    mine_weight = jnp.where(is_low, gate_weight, up_weight)
    slices = [
        lax.dynamic_slice_in_dim(mine_weight, place * SLICE, SLICE, 1)
        for place in (z, (z + 1) & 3, (z + 3) & 3, (z + 2) & 3)
    ]
    g_mine = lax.dynamic_index_in_dim(cotangent, core, 0, False)
    g_got = core_swap(lax.dynamic_index_in_dim(cotangent, 1 - core, 0, False))
    g_own = join([g_mine, g_got])
    wo = lax.all_gather(output_weight, "fsdp", axis=0, tiled=True)
    came = [slices[0]] + [move(piece) for move, piece in zip(Z_RING, slices[1:])]
    line = join(ring_gather(kv, FIRST_RING))
    g_blocks = direct_gather(g_own, Z_RING)
    sources = ring_gather(line, SECOND_RING)
    normed_swapped = core_swap(normed_one)

    attended, ox, lse = attend(order, queries, sources)

    x = jnp.concatenate([x_mine, x_got], axis=0).astype(F32)
    middle = x + dot(attended, wo)
    gain_two = gain_rows[1]
    scale_two = lax.rsqrt(jnp.mean(middle * middle, axis=-1, keepdims=True) + EPSILON)
    normed_two = (middle * scale_two * gain_two).astype(BF16)

    came, g_blocks = after((came, g_blocks), normed_two)
    mine_columns = place_rows(came, z)
    got_columns = core_swap(mine_columns)
    gate_up = jnp.where(
        is_low,
        jnp.concatenate([mine_columns, got_columns], axis=1),
        jnp.concatenate([got_columns, mine_columns], axis=1),
    )
    g_near, g_far = join(g_blocks[:3]), g_blocks[3]
    n_blocks = ring_gather(normed_two, Z_RING)
    n_near = join(n_blocks[:3])
    n_far = jnp.concatenate(n_blocks[3:], axis=0)

    def feed(n_rows, g_rows):
        gate_rows = dot(n_rows, gate_up[:, :SLICE])
        upper = dot(n_rows, gate_up[:, SLICE:])
        sigmoid_gate = jax.nn.sigmoid(gate_rows)
        hidden = (gate_rows * sigmoid_gate * upper).astype(BF16)
        grad_hidden = dot(g_rows, down_weight, NT)
        grad_gate = (
            grad_hidden * upper * sigmoid_gate * (1.0 + gate_rows * (1.0 - sigmoid_gate))
        ).astype(BF16)
        grad_upper = (grad_hidden * gate_rows * sigmoid_gate).astype(BF16)
        grad_both = jnp.concatenate([grad_gate, grad_upper], axis=1)
        return hidden, grad_both, dot(grad_both, gate_up, NT).astype(BF16)

    half = rows // 2
    hidden_near, both_near, back_near = feed(n_near, g_near)
    hidden_far, both_far, back_far = feed(n_far, g_far)
    near_grads = dot(n_near, both_near, TN), dot(g_near, hidden_near, TN)
    came = after(scatter_sends(back_far[:half], back_far[half:], Z_RING), *near_grads)
    terms = scatter_adds(back_near[:rows], back_near[rows : 2 * rows], back_near[2 * rows :], *came)
    both_tied, hidden_tied = after((both_far, hidden_far), *terms)
    both_grad = (near_grads[0] + dot(n_far, both_tied, TN)).astype(BF16)
    down_grad = (near_grads[1] + dot(g_far, hidden_tied, TN)).astype(BF16)
    came = after((Z_RING[1](terms[1]), Z_RING[0](terms[2])), both_grad, down_grad)
    grad_normed_two = terms[0].astype(F32) + came[0].astype(F32) + came[1].astype(F32)

    down_near, down_far = dot(hidden_near, down_weight).astype(BF16), dot(hidden_far, down_weight).astype(BF16)

    down_near, down_far = after((down_near, down_far), grad_normed_two)
    down_came = scatter_sends(down_far[:half], down_far[half:], Z_RING)
    norm_two_back = norm_back(grad_normed_two, middle, scale_two, gain_two)
    grad_middle = g_own.astype(F32) + norm_two_back
    grad_branch = grad_middle.astype(BF16)
    grad_attended = dot(grad_branch, wo, NT).astype(BF16)
    (grad_attended,) = after((grad_attended,), both_grad, down_grad, down_near, down_far)
    left_mine = jnp.where(is_low, normed_one, attended)
    left_got = core_swap(jnp.where(is_low, attended, normed_one))

    dq, *dkv = attend_back(order, queries, grad_attended, ox, lse, sources)

    def split(array):
        cuts = [0, rows, 2 * rows, 3 * rows, 3 * rows + half, 4 * rows]
        return [array[a:b] for a, b in zip(cuts[:-1], cuts[1:])]


    down_came, dq, *dkv = after((down_came, dq, *dkv))
    kv_came = scatter_sends(dkv[3], dkv[4], SECOND_RING)
    down_terms = scatter_adds(
        down_near[:rows], down_near[rows : 2 * rows], down_near[2 * rows :], *down_came
    )
    down_came = Z_RING[1](down_terms[1]), Z_RING[0](down_terms[2])
    grads = jnp.concatenate([both_grad, down_grad], axis=1).reshape(SIDE, SHARD // 8, 8, 3 * SLICE)
    grads = jnp.pad(grads, ((0, 0), (0, 2), (0, 0), (0, 0)))
    grads = grads.reshape(SIDE, SIDE, SIDE, 2, 8, 3 * SLICE)
    low_rows = grads[:, :, :, 0].transpose(2, 1, 0, 3, 4).reshape(2 * PADDED, 3 * SLICE)
    high_rows = grads[:, :, :, 1].transpose(1, 2, 0, 3, 4).reshape(2 * PADDED, 3 * SLICE)
    dense_mine = jnp.where(is_low, low_rows, high_rows)
    dense_got = core_swap(jnp.where(is_low, high_rows, low_rows))
    q_low = call(
        query_back_kernel, "query_back", jax.ShapeDtypeStruct((rows, D), BF16),
        (dq, cosine, sine), [VMEM] * 3,
    )
    right_mine = jnp.where(is_low, q_low, grad_branch)
    right_got = core_swap(jnp.where(is_low, grad_branch, q_low))
    kv_came, down_came, dense_mine, dense_got, right_got = together(
        kv_came, down_came, dense_mine, dense_got, right_got
    )

    kv_terms = scatter_adds(*dkv[:3], *kv_came)
    kv_came = SECOND_RING[1](kv_terms[1]), SECOND_RING[0](kv_terms[2])
    dense_mine = add_low(dense_mine, dense_got)
    blocks = [rows_at(dense_mine, place, PADDED // 2) for place in line_places]
    dense_came = scatter_sends(blocks[3][: PADDED // 4], blocks[3][PADDED // 4 :], FIRST_RING)
    square = (dot(left_mine, right_mine, TN) + dot(left_got, right_got, TN)).astype(BF16)
    square_blocks = [rows_at(square, place, SHARD) for place in ring_places]
    square_came = scatter_sends(
        square_blocks[3][: SHARD // 2], square_blocks[3][SHARD // 2 :], Z_RING
    )
    kv_came, dense_came, square_came = together(kv_came, dense_came, square_came)

    line = (kv_terms[0].astype(F32) + kv_came[0].astype(F32) + kv_came[1].astype(F32)).astype(BF16)
    line = split(line)
    kv_came = scatter_sends(line[3], line[4], FIRST_RING)
    dense_terms = scatter_adds(*blocks[:3], *dense_came)
    dense_came = FIRST_RING[1](dense_terms[1]), FIRST_RING[0](dense_terms[2])
    square_terms = scatter_adds(*square_blocks[:3], *square_came)
    square_came = Z_RING[1](square_terms[1]), Z_RING[0](square_terms[2])
    kv_came, dense_came = together(kv_came, dense_came)

    dense_line = sum(term.astype(F32) for term in (dense_terms[0], *dense_came)).astype(BF16)
    groups = [[ctx_index(y, x, 0) for y in range(SIDE)] for x in range(SIDE)]
    groups += [[ctx_index(y, x, 1) for x in range(SIDE)] for y in range(SIDE)]
    dense_sums = lax.psum_scatter(
        dense_line, "ctx", scatter_dimension=0, tiled=True, axis_index_groups=groups
    )
    kv_terms = scatter_adds(*line[:3], *kv_came)
    kv_came = FIRST_RING[1](kv_terms[1]), FIRST_RING[0](kv_terms[2])
    kv_came, square_came = together(kv_came, square_came)

    dkv_own = kv_terms[0].astype(F32) + kv_came[0].astype(F32) + kv_came[1].astype(F32)
    kv_low = call(
        kv_back_kernel, "kv_back", jax.ShapeDtypeStruct((rows, KV), BF16),
        (dkv_own, cosine, sine), [VMEM] * 3,
    )
    low_mine = lax.dynamic_slice_in_dim(kv_low, core * SIDE_AT, SIDE_COLUMNS, 1)
    low_got = core_swap(lax.dynamic_slice_in_dim(kv_low, (1 - core) * SIDE_AT, SIDE_COLUMNS, 1))
    square = sum(term.astype(F32) for term in (square_terms[0], *square_came)).astype(BF16)
    square = jnp.pad(square, ((0, PADDED - SHARD), (0, 0)))
    quarters = [rows_at(square, place, PADDED // 4) for place in line_places]
    square_came = scatter_sends(quarters[3][:32], quarters[3][32:], FIRST_RING)
    input_rows = call(
        input_back_kernel,
        "input_back",
        jax.ShapeDtypeStruct((rows, D), F32),
        (x_mine, x_got, kv_low, q_low, weight, gain_rows, grad_middle),
        [VMEM] * 7,
        flops=4 * 10**9,
    )
    input_low = input_rows.astype(BF16)
    low_got, square_came, dense_sums, input_low = together(low_got, square_came, dense_sums, input_low)

    side = (dot(normed_one, low_mine, TN) + dot(normed_swapped, low_got, TN)).astype(BF16)
    blocks = [rows_at(side, place, SHARD) for place in ring_places]
    side_came = scatter_sends(blocks[3][: SHARD // 2], blocks[3][SHARD // 2 :], Z_RING)
    square_terms = scatter_adds(*quarters[:3], *square_came)
    square_came = FIRST_RING[1](square_terms[1]), FIRST_RING[0](square_terms[2])
    dense_blocks = [
        rows_at(dense_sums[:, : 2 * SLICE], place, 8)
        for place in (z, (z + 1) & 3, (z + 3) & 3, (z + 2) & 3)
    ]
    dense_blocks = [dense_blocks[0]] + [move(block) for move, block in zip(Z_RING, dense_blocks[1:])]
    side_came, square_came, dense_blocks = together(side_came, square_came, dense_blocks)

    dense_blocks = list(dense_blocks)
    dense_blocks += [rows_at(dense_sums[:, 2 * SLICE :], place, 8) for place in range(SIDE)]
    dense_sums = lax.all_gather(
        jnp.concatenate(dense_blocks, axis=1), "ctx", axis=0, tiled=True
    )
    side_terms = scatter_adds(*blocks[:3], *side_came)
    side_came = Z_RING[1](side_terms[1]), Z_RING[0](side_terms[2])
    quarter = sum(term.astype(F32) for term in (square_terms[0], *square_came)).astype(BF16)
    quarters = direct_gather(quarter, SECOND_RING)
    side_came, quarters = together(side_came, quarters)

    side = sum(term.astype(F32) for term in (side_terms[0], *side_came)).astype(BF16)
    sides = direct_gather(side, FIRST_RING)
    quarter = sum(term.astype(F32) for term in quarters).astype(BF16)
    quarters = direct_gather(quarter, FIRST_RING)
    input_got = core_swap(input_low[tokens:])
    sides, quarters, input_got = together(sides, quarters, input_got)

    side = sum(term.astype(F32) for term in sides).astype(BF16)
    sides = direct_gather(side, SECOND_RING)
    square = place_rows(quarters, first_place)
    square_got = core_swap(square)
    sides, square_got = together(sides, square_got)
    side = sum(term.astype(F32) for term in sides).astype(BF16)
    side_got = core_swap(side)

    query_grad, key_grad, value_grad, output_grad, attend_total = call(
        finish_kernel, "finish",
        (
            jax.ShapeDtypeStruct((SHARD, D), F32),
            jax.ShapeDtypeStruct((SHARD, KV_HEADS * HEAD), F32),
            jax.ShapeDtypeStruct((SHARD, KV_HEADS * HEAD), F32),
            jax.ShapeDtypeStruct((SHARD, D), F32),
            jax.ShapeDtypeStruct((SHARD, 128), F32),
        ),
        (
            core.reshape(1).astype(jnp.int32), square, square_got, side, side_got,
            query_weight, key_weight, value_weight,
            jnp.broadcast_to(attend_gain.astype(F32)[:, None], (SHARD, 128)),
        ),
        [SMEM] + [VMEM] * 8,
    )
    wide = jax.ShapeDtypeStruct((SHARD, FF), F32)
    gain_column = jnp.broadcast_to(dense_gain.astype(F32)[:, None], (SHARD, 128))
    gate_grad, up_grad, down_grad, dense_total = call(
        unpack_kernel, "unpack",
        (
            wide, wide, jax.ShapeDtypeStruct((D, SLICE), F32),
            jax.ShapeDtypeStruct((SHARD, 128), F32),
        ),
        (z.reshape(1).astype(jnp.int32), dense_sums, gate_weight, up_weight, gain_column),
        [SMEM] + [VMEM] * 4,
    )

    def back_to_cores(keep, got):
        return jnp.where(is_low, jnp.stack([keep, got]), jnp.stack([got, keep]))

    layer_rows = sum(term.astype(F32) for term in (down_terms[0], *down_came))
    layer_rows = (middle + layer_rows).astype(BF16)
    return (
        back_to_cores(layer_rows[:tokens], core_swap(layer_rows[tokens:])),
        back_to_cores(input_low[:tokens], input_got).astype(F32),
        attend_total[:, 0],
        query_grad,
        key_grad,
        value_grad,
        output_grad,
        dense_total[:, 0],
        gate_grad,
        up_grad,
        down_grad.T,
    )


def solution(mesh):
    tokens = P("fsdp", "ctx", None)
    gain, weight = P("fsdp"), P("fsdp", None)
    weights = (gain, weight, weight, weight, weight, gain, weight, weight, weight)
    return jax.shard_map(
        local,
        mesh=mesh,
        in_specs=(tokens, tokens, P()) + weights,
        out_specs=(tokens, tokens) + weights,
        check_vma=False,
    )
```

```python
import functools

import jax
import jax.numpy as jnp
import numpy as np
from jax import lax
from jax.experimental import pallas as pl
from jax.experimental.pallas import tpu as pltpu
from jax.sharding import PartitionSpec as P

D = 960
FF = 2560
HEADS = 15
KV_HEADS = 5
GROUP = 3
HEAD = 64
HALF = 64
CHUNK = 256
SIDE = 4
KV = KV_HEADS * 128
PROJ = KV + D
PART = 832
PART_AT = PROJ - PART
SHARD = D // SIDE
PADDED = 256
SLICE = FF // SIDE
SIDE_COLUMNS = 384
SIDE_AT = KV - SIDE_COLUMNS
EPSILON = 1e-05
THETA = 100000.0
SCALE = 0.125
MASKED = -1e30
F32 = jnp.float32
BF16 = jnp.bfloat16
NN = (((1,), (0,)), ((), ()))
NT = (((1,), (1,)), ((), ()))
TN = (((0,), (0,)), ((), ()))
LIMIT = 52 * 2**20
SMEM = pl.BlockSpec(memory_space=pltpu.SMEM)
VMEM = pl.BlockSpec(memory_space=pltpu.VMEM)


def dot(left, right, dims=NN):
    return lax.dot_general(left, right, dims, preferred_element_type=F32)


def call(kernel, name, out_shape, inputs, in_specs, scratch=(), flops=10**9):
    return pl.pallas_call(
        kernel,
        out_shape=out_shape,
        in_specs=in_specs,
        out_specs=jax.tree.map(lambda _: VMEM, out_shape),
        scratch_shapes=list(scratch),
        compiler_params=pltpu.CompilerParams(vmem_limit_bytes=LIMIT),
        cost_estimate=pl.CostEstimate(flops=flops, bytes_accessed=0 if flops == 0 else 2**20, transcendentals=0),
        name=name,
    )(*inputs)


def join_kernel(*refs):
    first = 0
    for ref in refs[:-1]:
        refs[-1][first : first + ref.shape[0], :] = ref[...]
        first += ref.shape[0]


def join(pieces):
    rows = sum(piece.shape[0] for piece in pieces)
    shape = jax.ShapeDtypeStruct((rows, pieces[0].shape[1]), pieces[0].dtype)
    return call(join_kernel, "join", shape, tuple(pieces), [VMEM] * len(pieces))


def ctx_index(y, x, core):
    return (y * SIDE + x) * 2 + core


def plane_pairs(step, first_turn):
    pairs = []
    for y in range(SIDE):
        for x in range(SIDE):
            for core in range(2):
                along_x = (core == 0) == first_turn
                target = (y, (x + step) % SIDE) if along_x else ((y + step) % SIDE, x)
                pairs.append((ctx_index(y, x, core), ctx_index(*target, core)))
    return pairs


def z_move(step):
    pairs = [(z, (z + step) % SIDE) for z in range(SIDE)]
    return lambda rows: lax.ppermute(rows, "fsdp", pairs)


def plane_move(step, first_turn):
    pairs = plane_pairs(step, first_turn)
    return lambda rows: lax.ppermute(rows, "ctx", pairs)


def core_swap(rows):
    pairs = [(index, index ^ 1) for index in range(2 * SIDE * SIDE)]
    return lax.ppermute(rows, "ctx", pairs)


Z_RING = (z_move(1), z_move(-1), z_move(2))
FIRST_RING = (plane_move(1, True), plane_move(-1, True), plane_move(2, True))
SECOND_RING = (plane_move(1, False), plane_move(-1, False), plane_move(2, False))


def ring_gather(rows, ring):
    plus, minus, _ = ring
    half = rows.shape[0] // 2
    before, after = plus(rows), minus(rows)
    return rows, before, after, plus(before[:half]), minus(after[half:])


def direct_gather(rows, ring):
    return (rows, *(move(rows) for move in ring))


def add_low(left, right):
    return (left.astype(F32) + right.astype(F32)).astype(BF16)


def scatter_sends(opposite_top, opposite_low, ring):
    return ring[1](opposite_top), ring[0](opposite_low)


def scatter_adds(own, before, after_it, to_before, to_after):
    half = own.shape[0] // 2
    before = jnp.concatenate([add_low(before[:half], to_before), before[half:]], axis=0)
    after_it = jnp.concatenate([after_it[:half], add_low(after_it[half:], to_after)], axis=0)
    return own, before, after_it


def scatter_start(own, before, after_it, opposite_top, opposite_low, ring):
    return scatter_adds(own, before, after_it, *scatter_sends(opposite_top, opposite_low, ring))


def scatter_end(terms, ring):
    own, before, after_it = terms
    return own.astype(F32) + ring[1](before).astype(F32) + ring[0](after_it).astype(F32)


def ring_scatter(own, before, after_it, opposite_top, opposite_low, ring):
    return scatter_end(scatter_start(own, before, after_it, opposite_top, opposite_low, ring), ring)


def slot_table():
    devices = 2 * SIDE * SIDE
    held = {i: [2 * i, 2 * i + 1, 2 * (i ^ 1), 2 * (i ^ 1) + 1] for i in range(devices)}
    own = {i: list(held[i]) for i in held}
    for turn in (True, False):
        source = {step: {t: s for s, t in plane_pairs(step, turn)} for step in (1, -1, 2)}
        grown = {}
        for i in held:
            half = len(held[i]) // 2
            opposite = held[source[2][i]]
            grown[i] = (
                held[i] + held[source[1][i]] + held[source[-1][i]] + opposite[:half] + opposite[half:]
            )
        held = grown
    table = np.array([held[i] for i in range(devices)], np.int32)
    assert all((table[i, :4] == own[i]).all() for i in range(devices))
    return table


def pack_kernel(core_ref, q_ref, k_ref, v_ref, gain_one_ref, gain_two_ref, mine_ref, other_ref):
    columns = []
    for head in range(KV_HEADS):
        at = slice(head * HEAD, (head + 1) * HEAD)
        columns += [k_ref[:, at], v_ref[:, at]]
    columns.append(q_ref[...])
    packed = jnp.concatenate(columns, axis=1)
    low, high = packed[:, :PART], packed[:, PART_AT:]
    is_low = core_ref[0] == 0
    mine_ref[:SHARD, :] = jnp.where(is_low, low, high)
    other_ref[:SHARD, :] = jnp.where(is_low, high, low)
    rows = [gain_one_ref[...], gain_two_ref[...], jnp.zeros((PADDED - SHARD - 2, SHARD), BF16)]
    gains = jnp.concatenate([row.astype(F32) for row in rows], axis=0).astype(BF16)
    gains = jnp.concatenate([gains, jnp.zeros((PADDED - SHARD, PART - SHARD), BF16)], axis=1)
    mine_ref[SHARD:, :] = gains
    other_ref[SHARD:, :] = gains


def rope(values, cosine, sine, back):
    lane = lax.broadcasted_iota(jnp.int32, values.shape, 1)
    first = (lane & (HEAD - 1)) < HEAD // 2
    turned = values * sine if back else values
    ahead, behind = pltpu.roll(turned, 128 - HEAD // 2, 1), pltpu.roll(turned, HEAD // 2, 1)
    if back:
        return values * cosine + jnp.where(first, ahead, -behind)
    return values * cosine + jnp.where(first, -ahead, behind) * sine


def half_tables(cosine, sine):
    lane = lax.broadcasted_iota(jnp.int32, cosine.shape, 1)
    return jnp.where(lane < HEAD, cosine, 1.0), jnp.where(lane < HEAD, sine, 0.0)


def project_kernel(
    where_ref, x_mine, x_got, cosine_ref, sine_ref, *refs
):
    pieces, (q_ref, kv_ref, normed_ref, weight_ref, gains_ref, result) = refs[:10], refs[10:]
    z, core = where_ref[0], where_ref[1]
    mine_at = pl.multiple_of(core * PART_AT, 128)
    other_at = pl.multiple_of((1 - core) * PART_AT, 128)
    came = []
    for turn, place in enumerate((z, (z + 3) & 3, (z + 1) & 3)):
        at = pl.multiple_of(place * SHARD, 16)
        for piece, column in ((pieces[2 * turn], mine_at), (pieces[2 * turn + 1], other_at)):
            weight_ref[pl.ds(at, SHARD), pl.ds(column, PART)] = piece[:SHARD, :]
        came.append((place, pieces[2 * turn][SHARD:, :SHARD].astype(F32)))
    at = pl.multiple_of(((z + 2) & 3) * SHARD, 16)
    for top, low, column in ((pieces[6], pieces[8], mine_at), (pieces[7], pieces[9], other_at)):
        weight_ref[pl.ds(at, 128), pl.ds(column, PART)] = top[...]
        weight_ref[pl.ds(at + 128, SHARD - 128), pl.ds(column, PART)] = low[: SHARD - 128, :]
    came.append(((z + 2) & 3, pieces[8][SHARD - 128 :, :SHARD].astype(F32)))
    wide = jnp.concatenate(
        [sum(jnp.where(at == place, gain, 0.0) for at, gain in came) for place in range(SIDE)], axis=1
    )[:2]
    gains_ref[...] = wide
    rows = x_mine.shape[0]
    for half, x_ref in enumerate((x_mine, x_got)):
        x = x_ref[...].astype(F32)
        scale = lax.rsqrt(jnp.mean(x * x, axis=-1, keepdims=True) + EPSILON)
        normed_ref[half * rows : (half + 1) * rows, :] = (x * scale * wide[0:1]).astype(BF16)
    result[...] = dot(normed_ref[...], weight_ref[...])
    cosine, sine = cosine_ref[...], sine_ref[...]
    kv_tables = half_tables(cosine, sine)
    for head in range(KV_HEADS):
        at = slice(head * 128, (head + 1) * 128)
        kv_ref[:, at] = rope(result[:, at], *kv_tables, False).astype(BF16)
    for tile in range(D // 128):
        at = slice(tile * 128, (tile + 1) * 128)
        turned = rope(result[:, KV + tile * 128 : KV + (tile + 1) * 128], cosine, sine, False)
        q_ref[:, at] = (turned.astype(BF16) * SCALE).astype(BF16)
    tail = jnp.concatenate([result[:, PROJ - HEAD :]] * 2, axis=1)
    q_ref[:, D - HEAD :] = (rope(tail, cosine, sine, False)[:, :HEAD].astype(BF16) * SCALE).astype(
        BF16
    )


def sort_rows(order_ref, sources, sorted_ref):
    first = 0
    for source in sources:

        def step(slot, carry, source=source, first=first):
            place = order_ref[first + slot]
            sorted_ref[pl.ds(pl.multiple_of(place * HALF, HALF), HALF), :] = source[
                pl.ds(pl.multiple_of(slot * HALF, HALF), HALF), :
            ]
            return carry

        count = source.shape[0] // HALF
        lax.fori_loop(0, count, step, 0)
        first += count


def allowed_mask(chunk, place, rows):
    key_at = lax.broadcasted_iota(jnp.int32, (rows, CHUNK), 1) + chunk * CHUNK
    query_at = (lax.broadcasted_iota(jnp.int32, (rows, CHUNK), 0) & (HALF - 1)) + place * HALF
    return key_at <= query_at


def packed_queries(rows_ref, block, kv_head, upper):
    parts = []
    for member in range(GROUP):
        head = kv_head * GROUP + member
        part = rows_ref[block * HALF : (block + 1) * HALF, head * HEAD : (head + 1) * HEAD]
        zero = jnp.zeros_like(part)
        parts.append(jnp.concatenate([zero, part] if upper else [part, zero], axis=1))
    return jnp.concatenate(parts, axis=0)


def attend_kernel(blocks, parts, order_ref, q_ref, *refs):
    sources, (o_ref, ox_ref, lse_ref, kvs, qx, scores, tops) = refs[:parts], refs[parts:]
    rows = GROUP * HALF
    sort_rows(order_ref, sources, kvs)
    for block in range(blocks):
        for k in range(KV_HEADS):
            qx[block, k] = packed_queries(q_ref, block, k, False)

    def one_block(block, carry):
        place = order_ref[block]
        last = place >> 2
        tops[...] = jnp.full(tops.shape, MASKED, F32)

        def score_chunk(chunk, masked):
            at = pl.ds(pl.multiple_of(chunk * CHUNK, CHUNK), CHUNK)
            if masked:
                mask = allowed_mask(chunk, place, rows)
            for k in range(KV_HEADS):
                s = dot(qx[block, k], kvs[at, k * 128 : (k + 1) * 128], NT)
                if masked:
                    s = jnp.where(mask, s, MASKED)
                scores[k, chunk] = s
                tops[k] = jnp.maximum(tops[k], jnp.maximum(s[:, :128], s[:, 128:]))

        def score_step(chunk, c):
            score_chunk(chunk, False)
            return c

        lax.fori_loop(0, last, score_step, 0)
        score_chunk(last, True)
        for k in range(KV_HEADS):
            top = jnp.max(tops[k], axis=1, keepdims=True)
            tops[k] = jnp.broadcast_to(top, (rows, 128))
            lse_ref[block, k] = jnp.zeros((rows, 128), F32)
            ox_ref[block, k] = jnp.zeros((rows, 128), F32)

        def out_step(chunk, c):
            at = pl.ds(pl.multiple_of(chunk * CHUNK, CHUNK), CHUNK)
            for k in range(KV_HEADS):
                top = tops[k]
                s = scores[k, chunk]
                p0 = jnp.exp(s[:, :128] - top)
                p1 = jnp.exp(s[:, 128:] - top)
                lse_ref[block, k] += p0 + p1
                p = jnp.concatenate([p0, p1], axis=1).astype(BF16)
                ox_ref[block, k] += dot(p, kvs[at, k * 128 : (k + 1) * 128])
            return c

        lax.fori_loop(0, last + 1, out_step, 0)
        for k in range(KV_HEADS):
            total = jnp.sum(lse_ref[block, k], axis=1, keepdims=True)
            ox_ref[block, k] = ox_ref[block, k] / total
            lse_ref[block, k] = tops[k] + jnp.log(total)
        return carry

    lax.fori_loop(0, blocks, one_block, 0)
    for block in range(blocks):
        pieces = [
            ox_ref[block, k, g * HALF : (g + 1) * HALF, HEAD:].astype(BF16)
            for k in range(KV_HEADS)
            for g in range(GROUP)
        ]
        o_ref[block * HALF : (block + 1) * HALF, :] = jnp.concatenate(pieces, axis=1)


def attend(order, q, sources):
    length = sum(source.shape[0] for source in sources)
    blocks = q.shape[0] // HALF
    rows = GROUP * HALF
    packed = jax.ShapeDtypeStruct((blocks, KV_HEADS, rows, 128), F32)
    return call(
        functools.partial(attend_kernel, blocks, len(sources)),
        "attend",
        (jax.ShapeDtypeStruct(q.shape, BF16), packed, packed),
        (order, q, *sources),
        [SMEM] + [VMEM] * (1 + len(sources)),
        [
            pltpu.VMEM((length, KV), BF16),
            pltpu.VMEM((blocks, KV_HEADS, rows, 128), BF16),
            pltpu.VMEM((KV_HEADS, length // CHUNK, rows, CHUNK), F32),
            pltpu.VMEM((KV_HEADS, rows, 128), F32),
        ],
        3 * 10**10,
    )


def attend_back_kernel(
    blocks, parts, order_ref, q_ref, g_ref, ox_ref, lse_ref, *refs
):
    sources, refs = refs[:parts], refs[parts:]
    dq_ref, refs = refs[0], refs[1:]
    results, (kvs, qg, qgt, dots, dqx, dkvt) = refs[:parts], refs[parts:]
    rows = GROUP * HALF
    sort_rows(order_ref, sources, kvs)
    for block in range(blocks):
        for k in range(KV_HEADS):
            q = packed_queries(q_ref, block, k, False)
            g = packed_queries(g_ref, block, k, True)
            qg[block, k, :rows, :] = q
            qg[block, k, rows:, :] = g
            both = jnp.concatenate([q, g], axis=0).astype(F32)
            qgt[block, k] = both.T.astype(BF16)
            summed = jnp.sum(g.astype(F32) * ox_ref[block, k], axis=1, keepdims=True)
            dots[block, k] = jnp.broadcast_to(summed, (rows, 128))
    dqx[...] = jnp.zeros(dqx.shape, F32)

    def clear(chunk, c):
        dkvt[chunk] = jnp.zeros(dkvt.shape[1:], F32)
        return c

    lax.fori_loop(0, dkvt.shape[0], clear, 0)

    def one_block(block, carry):
        place = order_ref[block]
        last = place >> 2

        def chunk_work(chunk, masked):
            at = pl.ds(pl.multiple_of(chunk * CHUNK, CHUNK), CHUNK)
            if masked:
                mask = allowed_mask(chunk, place, rows)
            for k in range(KV_HEADS):
                keys = kvs[at, k * 128 : (k + 1) * 128]
                both = dot(qg[block, k], keys, NT)
                lse = lse_ref[block, k]
                dots_here = dots[block, k]
                ps, ds = [], []
                for half in range(2):
                    lanes = slice(half * 128, (half + 1) * 128)
                    p = jnp.exp(both[:rows, lanes] - lse)
                    if masked:
                        p = jnp.where(mask[:, lanes], p, 0.0)
                    ps.append(p.astype(BF16))
                    ds.append((p * (both[rows:, lanes] - dots_here)).astype(BF16))
                p = jnp.concatenate(ps, axis=1)
                d = jnp.concatenate(ds, axis=1)
                dqx[block, k] += dot(d, keys)
                dkvt[chunk, k] += dot(qgt[block, k], jnp.concatenate([d, p], axis=0))

        def step(chunk, c):
            chunk_work(chunk, False)
            return c

        lax.fori_loop(0, last, step, 0)
        chunk_work(last, True)
        return carry

    lax.fori_loop(0, blocks, one_block, 0)
    for block in range(blocks):
        pieces = [
            dqx[block, k, g * HALF : (g + 1) * HALF, :HEAD] * SCALE
            for k in range(KV_HEADS)
            for g in range(GROUP)
        ]
        dq_ref[block * HALF : (block + 1) * HALF, :] = jnp.concatenate(pieces, axis=1)

    def turn(chunk, c):
        at = pl.ds(pl.multiple_of(chunk * CHUNK, CHUNK), CHUNK)
        for k in range(KV_HEADS):
            kvs[at, k * 128 : (k + 1) * 128] = dkvt[chunk, k].T.astype(BF16)
        return c

    lax.fori_loop(0, dkvt.shape[0], turn, 0)
    first = 0
    for result in results:

        def unsort(slot, c, result=result, first=first):
            place = order_ref[first + slot]
            result[pl.ds(pl.multiple_of(slot * HALF, HALF), HALF), :] = kvs[
                pl.ds(pl.multiple_of(place * HALF, HALF), HALF), :
            ]
            return c

        count = result.shape[0] // HALF
        lax.fori_loop(0, count, unsort, 0)
        first += count


def attend_back(order, q, g, ox, lse, sources):
    length = sum(source.shape[0] for source in sources)
    blocks = q.shape[0] // HALF
    rows = GROUP * HALF
    return call(
        functools.partial(attend_back_kernel, blocks, len(sources)),
        "attend_back",
        (jax.ShapeDtypeStruct(q.shape, F32),)
        + tuple(jax.ShapeDtypeStruct(source.shape, BF16) for source in sources),
        (order, q, g, ox, lse, *sources),
        [SMEM] + [VMEM] * (4 + len(sources)),
        [
            pltpu.VMEM((length, KV), BF16),
            pltpu.VMEM((blocks, KV_HEADS, 2 * rows, 128), BF16),
            pltpu.VMEM((blocks, KV_HEADS, 128, 2 * rows), BF16),
            pltpu.VMEM((blocks, KV_HEADS, rows, 128), F32),
            pltpu.VMEM((blocks, KV_HEADS, rows, 128), F32),
            pltpu.VMEM((length // CHUNK, KV_HEADS, 128, CHUNK), F32),
        ],
        0,
    )


def query_back_kernel(dq_ref, cosine_ref, sine_ref, low_ref):
    cosine, sine = cosine_ref[...], sine_ref[...]
    for tile in range(D // 128):
        at = slice(tile * 128, (tile + 1) * 128)
        low_ref[:, at] = rope(dq_ref[:, at], cosine, sine, True).astype(BF16)
    tail = jnp.concatenate([dq_ref[:, D - HEAD :]] * 2, axis=1)
    low_ref[:, D - HEAD :] = rope(tail, cosine, sine, True)[:, :HEAD].astype(BF16)


def kv_back_kernel(dkv_ref, cosine_ref, sine_ref, low_ref):
    kv_tables = half_tables(cosine_ref[...], sine_ref[...])
    for head in range(KV_HEADS):
        at = slice(head * 128, (head + 1) * 128)
        low_ref[:, at] = rope(dkv_ref[:, at], *kv_tables, True).astype(BF16)


def input_back_kernel(
    x_mine, x_got, kv_low_ref, q_low_ref, weight_ref, gains_ref, middle_ref, grads_ref
):
    back = dot(kv_low_ref[...], weight_ref[:, :KV], NT) + dot(q_low_ref[...], weight_ref[:, KV:], NT)
    rows = x_mine.shape[0]
    gain = gains_ref[0:1, :]
    for half, x_ref in enumerate((x_mine, x_got)):
        at = slice(half * rows, (half + 1) * rows)
        x = x_ref[...].astype(F32)
        scale = lax.rsqrt(jnp.mean(x * x, axis=-1, keepdims=True) + EPSILON)
        unit = x * scale
        weighted = back[at] * gain
        inner = jnp.mean(weighted * unit, axis=-1, keepdims=True)
        grads_ref[at, :] = middle_ref[at, :] + scale * (weighted - unit * inner)


def place_kernel(own_ref, *refs):
    for piece, step in zip(refs[:-1], (0, 3, 1, 2)):
        rows = piece.shape[0]
        at = pl.multiple_of(((own_ref[0] + step) & 3) * rows, 16)
        refs[-1][pl.ds(at, rows), :] = piece[...]


def place_rows(pieces, own):
    rows, columns = pieces[0].shape
    shape = jax.ShapeDtypeStruct((SIDE * rows, columns), pieces[0].dtype)
    return call(
        place_kernel, "place", shape, (own.reshape(1).astype(jnp.int32), *pieces), [SMEM] + [VMEM] * 4
    )


def finish_kernel(
    core_ref, square_ref, square_got_ref, side_ref, side_got_ref, query_weight_ref, key_weight_ref,
    value_weight_ref, gain_ref, query_ref, key_ref, value_ref, output_ref, total_ref,
):
    is_low = core_ref[0] == 0
    mine, got = square_ref[:SHARD, :].astype(F32), square_got_ref[:SHARD, :].astype(F32)
    query = jnp.where(is_low, mine, got)
    query_ref[...] = query
    output_ref[...] = jnp.where(is_low, got, mine)
    mine, got = side_ref[...].astype(F32), side_got_ref[...].astype(F32)
    low, high = jnp.where(is_low, mine, got), jnp.where(is_low, got, mine)
    pairs = [low[:, at : at + 128] for at in range(0, SIDE_COLUMNS, 128)]
    pairs += [high[:, at : at + 128] for at in range(2 * SIDE_COLUMNS - KV, SIDE_COLUMNS, 128)]
    key = jnp.concatenate([pair[:, :HEAD] for pair in pairs], axis=1)
    value = jnp.concatenate([pair[:, HEAD:] for pair in pairs], axis=1)
    key_ref[...] = key.T
    value_ref[...] = value.T
    total = jnp.zeros((SHARD, 1), F32)
    for weight, grad in ((query_weight_ref, query), (key_weight_ref, key), (value_weight_ref, value)):
        total += jnp.sum(weight[...].astype(F32) * grad, axis=1, keepdims=True)
    total_ref[...] = jnp.broadcast_to(total, (SHARD, 128)) / gain_ref[...]


def unpack_kernel(
    z_ref, sums_ref, gate_weight_ref, up_weight_ref, gain_ref, gate_ref, up_ref, down_ref, dense_ref
):
    z = z_ref[0]
    for turn, step in enumerate((0, 3, 1, 2)):
        at = pl.ds(pl.multiple_of(((z + step) & 3) * SLICE, 128), SLICE)
        first = turn * 2 * SLICE
        gate_ref[:, at] = sums_ref[:SHARD, first : first + SLICE].astype(F32)
        up_ref[:, at] = sums_ref[:SHARD, first + SLICE : first + 2 * SLICE].astype(F32)
        columns = slice(2 * FF + turn * SLICE, 2 * FF + (turn + 1) * SLICE)
        down_ref[turn * SHARD : (turn + 1) * SHARD, :] = sums_ref[:SHARD, columns].astype(F32)
    terms = gate_weight_ref[...].astype(F32) * gate_ref[...] + up_weight_ref[...].astype(F32) * up_ref[...]
    total = jnp.sum(terms, axis=1, keepdims=True)
    dense_ref[...] = jnp.broadcast_to(total, (SHARD, 128)) / gain_ref[...]


def rope_angles(places):
    pair_ids = jnp.arange(HEAD // 2, dtype=F32)
    frequency = THETA ** (-2.0 * pair_ids / HEAD)
    return places.astype(F32)[:, None] * frequency[None, :]


def rope_tables(places):
    angles = rope_angles(places)
    return jnp.tile(jnp.cos(angles), (1, 4)), jnp.tile(jnp.sin(angles), (1, 4))


def norm_back(grad_normed, values, scale, gain):
    unit_rows = values * scale
    weighted = grad_normed * gain
    inner = jnp.mean(weighted * unit_rows, axis=-1, keepdims=True)
    return scale * (weighted - unit_rows * inner)


def together(*groups):
    return lax.optimization_barrier(groups)


def after(values, *others):
    return lax.optimization_barrier((tuple(values), others))[0]


def rows_at(array, block, size):
    return lax.dynamic_slice_in_dim(array, block * size, size, 0)


def local(
    activations, cotangent, block_order, attend_gain, query_weight, key_weight, value_weight,
    output_weight, dense_gain, gate_weight, up_weight, down_weight,
):
    index = lax.axis_index("ctx")
    z = lax.axis_index("fsdp")
    core = index & 1
    tokens = activations.shape[1]
    rows = 2 * tokens
    ring_places = (z, (z + 3) & 3, (z + 1) & 3, (z + 2) & 3)

    x_mine = lax.dynamic_index_in_dim(activations, core, 0, False)
    x_got = core_swap(lax.dynamic_index_in_dim(activations, 1 - core, 0, False))

    shape = jax.ShapeDtypeStruct((PADDED, PART), BF16)
    mine, other = call(
        pack_kernel, "pack", (shape, shape),
        (
            core.reshape(1).astype(jnp.int32), query_weight, key_weight, value_weight,
            attend_gain.reshape(1, SHARD), dense_gain.reshape(1, SHARD),
        ),
        [SMEM] + [VMEM] * 5,
    )
    ringed = ring_gather(mine, Z_RING)
    pieces = [mine, other]
    for piece in ringed[1:]:
        pieces += [piece, core_swap(piece)]

    slots = jnp.asarray(slot_table())[index]
    order = jnp.sum(
        jnp.where(slots[:, None] == jnp.arange(64, dtype=jnp.int32)[None, :], block_order[None, :], 0),
        axis=1,
    )
    places = (order[: rows // HALF, None] * HALF + jnp.arange(HALF, dtype=jnp.int32)).reshape(rows)
    cosine, sine = rope_tables(places)
    queries, kv, normed_one, weight, gain_rows = call(
        project_kernel,
        "project",
        (
            jax.ShapeDtypeStruct((rows, D), BF16),
            jax.ShapeDtypeStruct((rows, KV), BF16),
            jax.ShapeDtypeStruct((rows, D), BF16),
            jax.ShapeDtypeStruct((D, PROJ), BF16),
            jax.ShapeDtypeStruct((2, D), F32),
        ),
        (jnp.stack([z, core]).astype(jnp.int32), x_mine, x_got, cosine, sine, *pieces),
        [SMEM] + [VMEM] * 14,
        [pltpu.VMEM((rows, PROJ), F32)],
        5 * 10**9,
    )

    is_low = core == 0
    y, x_at = index >> 3, (index >> 1) & 3
    first_place = jnp.where(is_low, x_at, y)
    line_places = [(first_place + step) & 3 for step in (0, 3, 1, 2)]

    cotangent, output_weight, gate_weight, up_weight = after(
        (cotangent, output_weight, gate_weight, up_weight), kv
    )
    mine_weight = jnp.where(is_low, gate_weight, up_weight)
    slices = [
        lax.dynamic_slice_in_dim(mine_weight, place * SLICE, SLICE, 1)
        for place in (z, (z + 1) & 3, (z + 3) & 3, (z + 2) & 3)
    ]
    g_mine = lax.dynamic_index_in_dim(cotangent, core, 0, False)
    g_got = core_swap(lax.dynamic_index_in_dim(cotangent, 1 - core, 0, False))
    g_own = join([g_mine, g_got])
    wo = lax.all_gather(output_weight, "fsdp", axis=0, tiled=True)
    came = [slices[0]] + [move(piece) for move, piece in zip(Z_RING, slices[1:])]
    line = join(ring_gather(kv, FIRST_RING))
    came = after(came, line)
    mine_columns = place_rows(came, z)
    got_columns = core_swap(mine_columns)
    g_blocks = ring_gather(after((g_own,), line)[0], Z_RING)
    sources = ring_gather(line, SECOND_RING)
    gate_up = jnp.where(
        is_low,
        jnp.concatenate([mine_columns, got_columns], axis=1),
        jnp.concatenate([got_columns, mine_columns], axis=1),
    )
    normed_swapped = core_swap(normed_one)
    sources = after(sources, gate_up, normed_swapped)

    attended, ox, lse = attend(order, queries, sources)

    x = jnp.concatenate([x_mine, x_got], axis=0).astype(F32)
    middle = x + dot(attended, wo)
    gain_two = gain_rows[1]
    scale_two = lax.rsqrt(jnp.mean(middle * middle, axis=-1, keepdims=True) + EPSILON)
    normed_two = (middle * scale_two * gain_two).astype(BF16)

    n_blocks = ring_gather(normed_two, Z_RING)
    g_blocks = after(g_blocks, n_blocks[1], n_blocks[2])
    g_near, g_far = join(g_blocks[:3]), jnp.concatenate(g_blocks[3:], axis=0)
    n_near = join(n_blocks[:3])
    n_far = jnp.concatenate(n_blocks[3:], axis=0)

    def feed(n_rows, g_rows):
        gate_rows = dot(n_rows, gate_up[:, :SLICE])
        upper = dot(n_rows, gate_up[:, SLICE:])
        sigmoid_gate = jax.nn.sigmoid(gate_rows)
        hidden = (gate_rows * sigmoid_gate * upper).astype(BF16)
        grad_hidden = dot(g_rows, down_weight, NT)
        grad_gate = (
            grad_hidden * upper * sigmoid_gate * (1.0 + gate_rows * (1.0 - sigmoid_gate))
        ).astype(BF16)
        grad_upper = (grad_hidden * gate_rows * sigmoid_gate).astype(BF16)
        grad_both = jnp.concatenate([grad_gate, grad_upper], axis=1)
        return hidden, grad_both, dot(grad_both, gate_up, NT).astype(BF16)

    half = rows // 2
    hidden_near, both_near, back_near = feed(n_near, g_near)
    hidden_far, both_far, back_far = feed(n_far, g_far)
    near_grads = dot(n_near, both_near, TN), dot(g_near, hidden_near, TN)
    came = after(scatter_sends(back_far[:half], back_far[half:], Z_RING), *near_grads)
    terms = scatter_adds(back_near[:rows], back_near[rows : 2 * rows], back_near[2 * rows :], *came)
    both_tied, hidden_tied = after((both_far, hidden_far), *terms)
    both_grad = (near_grads[0] + dot(n_far, both_tied, TN)).astype(BF16)
    down_grad = (near_grads[1] + dot(g_far, hidden_tied, TN)).astype(BF16)
    came = after((Z_RING[1](terms[1]), Z_RING[0](terms[2])), both_grad, down_grad)
    grad_normed_two = terms[0].astype(F32) + came[0].astype(F32) + came[1].astype(F32)

    down_near, down_far = dot(hidden_near, down_weight).astype(BF16), dot(hidden_far, down_weight).astype(BF16)

    down_near, down_far = after((down_near, down_far), grad_normed_two)
    down_came = scatter_sends(down_far[:half], down_far[half:], Z_RING)
    grads = jnp.concatenate([both_grad, down_grad], axis=1).reshape(SIDE, SHARD // 8, 8, 3 * SLICE)
    grads = jnp.pad(grads, ((0, 0), (0, 2), (0, 0), (0, 0)))
    grads = grads.reshape(SIDE, SIDE, SIDE, 2, 8, 3 * SLICE)
    low_rows = grads[:, :, :, 0].transpose(2, 1, 0, 3, 4).reshape(2 * PADDED, 3 * SLICE)
    high_rows = grads[:, :, :, 1].transpose(1, 2, 0, 3, 4).reshape(2 * PADDED, 3 * SLICE)
    dense_mine = jnp.where(is_low, low_rows, high_rows)
    dense_got = core_swap(jnp.where(is_low, high_rows, low_rows))
    norm_two_back = norm_back(grad_normed_two, middle, scale_two, gain_two)
    grad_middle = g_own.astype(F32) + norm_two_back
    grad_branch = grad_middle.astype(BF16)
    grad_attended = dot(grad_branch, wo, NT).astype(BF16)
    (grad_attended,) = after((grad_attended,), both_grad, down_grad, down_near, down_far)
    left_mine = jnp.where(is_low, normed_one, attended)
    left_got = core_swap(jnp.where(is_low, attended, normed_one))

    dq, *dkv = attend_back(order, queries, grad_attended, ox, lse, sources)

    def split(array):
        cuts = [0, rows, 2 * rows, 3 * rows, 3 * rows + half, 4 * rows]
        return [array[a:b] for a, b in zip(cuts[:-1], cuts[1:])]


    down_came, dense_got, dq, *dkv = after((down_came, dense_got, dq, *dkv))
    dense_mine = add_low(dense_mine, dense_got)
    blocks = [rows_at(dense_mine, place, PADDED // 2) for place in line_places]
    dense_came = scatter_sends(blocks[3][: PADDED // 4], blocks[3][PADDED // 4 :], FIRST_RING)
    kv_came = scatter_sends(dkv[3], dkv[4], SECOND_RING)
    down_terms = scatter_adds(
        down_near[:rows], down_near[rows : 2 * rows], down_near[2 * rows :], *down_came
    )
    q_low = call(
        query_back_kernel, "query_back", jax.ShapeDtypeStruct((rows, D), BF16),
        (dq, cosine, sine), [VMEM] * 3,
    )
    right_mine = jnp.where(is_low, q_low, grad_branch)
    right_got = core_swap(jnp.where(is_low, grad_branch, q_low))
    square = (dot(left_mine, right_mine, TN) + dot(left_got, right_got, TN)).astype(BF16)
    kv_came, dense_came, square = together(kv_came, dense_came, square)

    kv_terms = scatter_adds(*dkv[:3], *kv_came)
    kv_came = SECOND_RING[1](kv_terms[1]), SECOND_RING[0](kv_terms[2])
    dense_terms = scatter_adds(*blocks[:3], *dense_came)
    dense_came = FIRST_RING[1](dense_terms[1]), FIRST_RING[0](dense_terms[2])
    kv_came, dense_came = together(kv_came, dense_came)

    line = (kv_terms[0].astype(F32) + kv_came[0].astype(F32) + kv_came[1].astype(F32)).astype(BF16)
    line = split(line)
    kv_came = scatter_sends(line[3], line[4], FIRST_RING)
    dense_line = sum(term.astype(F32) for term in (dense_terms[0], *dense_came)).astype(BF16)
    groups = [[ctx_index(y, x, 0) for y in range(SIDE)] for x in range(SIDE)]
    groups += [[ctx_index(y, x, 1) for x in range(SIDE)] for y in range(SIDE)]
    dense_sums = lax.psum_scatter(
        dense_line, "ctx", scatter_dimension=0, tiled=True, axis_index_groups=groups
    )
    square_blocks = [rows_at(square, place, SHARD) for place in ring_places]
    square_came = scatter_sends(
        square_blocks[3][: SHARD // 2], square_blocks[3][SHARD // 2 :], Z_RING
    )
    kv_came, square_came = together(kv_came, square_came)

    kv_terms = scatter_adds(*line[:3], *kv_came)
    kv_came = FIRST_RING[1](kv_terms[1]), FIRST_RING[0](kv_terms[2])
    square_terms = scatter_adds(*square_blocks[:3], *square_came)
    square_came = Z_RING[1](square_terms[1]), Z_RING[0](square_terms[2])
    kv_came, square_came, dense_sums = together(kv_came, square_came, dense_sums)

    dkv_own = kv_terms[0].astype(F32) + kv_came[0].astype(F32) + kv_came[1].astype(F32)
    kv_low = call(
        kv_back_kernel, "kv_back", jax.ShapeDtypeStruct((rows, KV), BF16),
        (dkv_own, cosine, sine), [VMEM] * 3,
    )
    low_mine = lax.dynamic_slice_in_dim(kv_low, core * SIDE_AT, SIDE_COLUMNS, 1)
    low_got = core_swap(lax.dynamic_slice_in_dim(kv_low, (1 - core) * SIDE_AT, SIDE_COLUMNS, 1))
    input_rows = call(
        input_back_kernel,
        "input_back",
        jax.ShapeDtypeStruct((rows, D), F32),
        (x_mine, x_got, kv_low, q_low, weight, gain_rows, grad_middle),
        [VMEM] * 7,
        flops=4 * 10**9,
    )
    input_low = input_rows.astype(BF16)
    dense_blocks = [
        rows_at(dense_sums[:, : 2 * SLICE], place, 8)
        for place in (z, (z + 1) & 3, (z + 3) & 3, (z + 2) & 3)
    ]
    dense_blocks = [dense_blocks[0]] + [move(block) for move, block in zip(Z_RING, dense_blocks[1:])]
    down_before = Z_RING[1](down_terms[1])
    low_got, dense_blocks, input_low, down_before = together(
        low_got, dense_blocks, input_low, down_before
    )

    def back_to_cores(keep, got):
        return jnp.where(is_low, jnp.stack([keep, got]), jnp.stack([got, keep])).transpose(0, 2, 1)

    input_got = core_swap(input_low[tokens:])

    side = (dot(normed_one, low_mine, TN) + dot(normed_swapped, low_got, TN)).astype(BF16)
    blocks = [rows_at(side, place, SHARD) for place in ring_places]
    side_came = scatter_sends(blocks[3][: SHARD // 2], blocks[3][SHARD // 2 :], Z_RING)
    square = sum(term.astype(F32) for term in (square_terms[0], *square_came)).astype(BF16)
    square = jnp.pad(square, ((0, PADDED - SHARD), (0, 0)))
    quarters = [rows_at(square, place, PADDED // 4) for place in line_places]
    square_came = scatter_sends(quarters[3][:32], quarters[3][32:], FIRST_RING)
    dense_blocks = list(dense_blocks)
    dense_blocks += [rows_at(dense_sums[:, 2 * SLICE :], place, 8) for place in range(SIDE)]
    dense_sums = lax.all_gather(
        jnp.concatenate(dense_blocks, axis=1), "ctx", axis=0, tiled=True
    )
    side_came, square_came, input_got = together(side_came, square_came, input_got)

    side_terms = scatter_adds(*blocks[:3], *side_came)
    side_came = Z_RING[1](side_terms[1]), Z_RING[0](side_terms[2])
    square_terms = scatter_adds(*quarters[:3], *square_came)
    square_came = FIRST_RING[1](square_terms[1]), FIRST_RING[0](square_terms[2])
    down_after = Z_RING[0](down_terms[2])
    side_came, square_came, down_after = together(side_came, square_came, down_after)

    side = sum(term.astype(F32) for term in (side_terms[0], *side_came)).astype(BF16)
    sides = direct_gather(side, FIRST_RING)
    quarter = sum(term.astype(F32) for term in (square_terms[0], *square_came)).astype(BF16)
    quarter_came = SECOND_RING[2](quarter)
    input_back = back_to_cores(input_low[:tokens], input_got).astype(F32)
    layer_rows = sum(term.astype(F32) for term in (down_terms[0], down_before, down_after))
    layer_rows = (middle + layer_rows).astype(BF16)
    layer_got = core_swap(layer_rows[tokens:])
    sides, quarter_came, input_back, layer_got = together(sides, quarter_came, input_back, layer_got)

    side = sum(term.astype(F32) for term in sides).astype(BF16)
    sides = direct_gather(side, SECOND_RING)
    quarter = add_low(quarter, quarter_came)
    quarter_came = SECOND_RING[0](quarter)
    layer_rows = back_to_cores(layer_rows[:tokens], layer_got)
    sides, quarter_came, layer_rows = together(sides, quarter_came, layer_rows)

    side = sum(term.astype(F32) for term in sides).astype(BF16)
    side_got = core_swap(side)
    quarters = direct_gather(add_low(quarter, quarter_came), FIRST_RING)
    wide = jax.ShapeDtypeStruct((SHARD, FF), F32)
    gain_column = jnp.broadcast_to(dense_gain.astype(F32)[:, None], (SHARD, 128))
    gate_grad, up_grad, down_grad, dense_total = call(
        unpack_kernel, "unpack",
        (
            wide, wide, jax.ShapeDtypeStruct((D, SLICE), F32),
            jax.ShapeDtypeStruct((SHARD, 128), F32),
        ),
        (z.reshape(1).astype(jnp.int32), dense_sums, gate_weight, up_weight, gain_column),
        [SMEM] + [VMEM] * 4,
    )

    side_got, quarters, gate_grad, up_grad, down_grad = together(
        side_got, quarters, gate_grad, up_grad, down_grad
    )
    square = place_rows(quarters, first_place)
    square_got = core_swap(square)

    query_grad, key_grad, value_grad, output_grad, attend_total = call(
        finish_kernel, "finish",
        (
            jax.ShapeDtypeStruct((SHARD, D), F32),
            jax.ShapeDtypeStruct((KV_HEADS * HEAD, SHARD), F32),
            jax.ShapeDtypeStruct((KV_HEADS * HEAD, SHARD), F32),
            jax.ShapeDtypeStruct((SHARD, D), F32),
            jax.ShapeDtypeStruct((SHARD, 128), F32),
        ),
        (
            core.reshape(1).astype(jnp.int32), square, square_got, side, side_got,
            query_weight, key_weight, value_weight,
            jnp.broadcast_to(attend_gain.astype(F32)[:, None], (SHARD, 128)),
        ),
        [SMEM] + [VMEM] * 8,
    )
    return (
        layer_rows.transpose(0, 2, 1),
        input_back.transpose(0, 2, 1),
        attend_total[:, 0],
        query_grad,
        key_grad.T,
        value_grad.T,
        output_grad,
        dense_total[:, 0],
        gate_grad,
        up_grad,
        down_grad.T,
    )


def solution(mesh):
    tokens = P("fsdp", "ctx", None)
    gain, weight = P("fsdp"), P("fsdp", None)
    weights = (gain, weight, weight, weight, weight, gain, weight, weight, weight)
    return jax.shard_map(
        local,
        mesh=mesh,
        in_specs=(tokens, tokens, P()) + weights,
        out_specs=(tokens, tokens) + weights,
        check_vma=False,
    )
```
